32 devices in a mesh: user: 16 (over z, y, core), item: 2 (over x).
Axes of the slice: x: 2, y: 2, z: 4, core: 2. Of those that a mesh axis runs over, the one named last changes fastest.
Arguments:
- observed: bfloat16 [32, 128, 128, 128], P(('user', 'item')), may hold values from -6 to 6
- user_block: int32 [32], P(('user', 'item')), may hold values from 0 to 3
- item_block: int32 [32], P(('user', 'item')), may hold values from 0 to 1
- stratum: int32 [32], P(('user', 'item')), may hold values from 0 to 1
- context_ids: int32 [32, 128], P(('user', 'item')), may hold values from 0 to 255
- core_tensor: float32 [16384, 128], P(('user', 'item')), may hold values from -1 to 1
- user_factor: bfloat16 [8192, 128], P('user'), may hold values from -3 to 3
- item_factor: bfloat16 [512, 128], P('item'), may hold values from -3 to 3
- context_factor: bfloat16 [256, 128], P(('user', 'item')), may hold values from -3 to 3
Outputs:
- core_grad: float32 [16384, 128], P(('user', 'item'))
- user_grad: float32 [8192, 128], P(('user', 'item'))
- item_grad: float32 [512, 128], P(('user', 'item'))
- context_grad: float32 [256, 128], P(('user', 'item'))
The draws below stay inside these ranges and needn't reach their ends.
Inputs may be any that keep to these rules, and one draw needn't show every extreme that they name: `user_block`: user block within the tile's user index.
All inputs are finite; a program needn't handle non-finite values.
Results may differ from the reference program's by a relative error of at most 0.0031.
Values may be sent and summed in bfloat16 or wider, within the bound.
A program may use at most 128 MiB of HBM per device.

```python
import math
import jax
import jax.numpy as jnp
from jax import lax

R1 = 128
R2 = 128
R3 = 128
BU = 128
BI = 128
KC = 128
TILES_DEV = 1
UB_DEV = 4
IB_DEV = 2
TILES = 32
NU = 8192
NI = 512
NC = 256
N_ITEM = 2


def set_ends(values, own_key, low, high):
    longest = values.shape.index(max(values.shape))
    spots = []
    for shift in (0, 1):
        where = [jax.random.randint(jax.random.fold_in(own_key, axis), (), 0, length) for axis, length in enumerate(values.shape)]
        where[longest] = (where[longest] + shift) % values.shape[longest]
        spots.append(tuple(where))
    return values.at[spots[0]].set(low).at[spots[1]].set(high)


def shard_levels(key, dims, shards, least, top_value):
    def one(dim, blocks):
        draws = jax.random.uniform(jax.random.fold_in(jax.random.fold_in(key, 6), dim), (blocks,), jnp.float32, least / len(shards), top_value / len(shards))
        return jnp.repeat(jnp.exp(draws), dims[dim] // blocks).reshape((-1,) + (1,) * (len(dims) - dim - 1))

    level = one(*shards[0])
    for cut in shards[1:]:
        level = level * one(*cut)
    return level


def normal_values(key, shape, scale, limit, shards=(), kind=jnp.bfloat16):
    gain = shard_levels(key, shape, shards, -0.22, 0.18) if shards else 1.0
    result = jax.random.normal(key, shape, jnp.float32) * scale * gain
    return jnp.minimum(jnp.maximum(result, -limit), limit).astype(kind)


def setup_inputs(seed: int = 0) -> dict:
    key_of = jax.random.split(jax.random.key(seed), 10)
    observed = normal_values(key_of[0], (TILES, BU, BI, KC), 1.0, 6.0, ((0, 32),))
    user_block = set_ends(jax.random.randint(key_of[1], (TILES,), 0, UB_DEV), jax.random.fold_in(key_of[1], 1), 0, UB_DEV - 1).astype(jnp.int32)
    item_block = set_ends(jax.random.randint(key_of[2], (TILES,), 0, IB_DEV), jax.random.fold_in(key_of[2], 1), 0, IB_DEV - 1).astype(jnp.int32)
    stratum = set_ends(jax.random.randint(key_of[3], (TILES,), 0, N_ITEM), jax.random.fold_in(key_of[3], 1), 0, N_ITEM - 1).astype(jnp.int32)
    context_ids = set_ends(jax.random.randint(key_of[4], (TILES, KC), 0, NC), jax.random.fold_in(key_of[4], 1), 0, NC - 1).astype(jnp.int32)
    core_tensor = normal_values(key_of[5], (R1 * R2, R3), 0.074, 1.0, ((0, 32),), jnp.float32)
    user_factor = normal_values(key_of[6], (NU, R1), 0.21, 3.0, ((0, 16),))
    item_factor = normal_values(key_of[7], (NI, R2), 0.21, 3.0, ((0, 2),))
    context_factor = normal_values(key_of[8], (NC, R3), 0.21, 3.0, ((0, 32),))
    return dict(observed=observed, user_block=user_block, item_block=item_block, stratum=stratum, context_ids=context_ids, core_tensor=core_tensor, user_factor=user_factor, item_factor=item_factor, context_factor=context_factor)


def tile_terms(core_half, user_rows, item_rows, ctx_rows, observed_tile):
    first_pass = jnp.dot(core_half, ctx_rows.T, preferred_element_type=jnp.float32).astype(jnp.bfloat16)
    first_cube = first_pass.reshape(R1, R2, KC)
    second = jnp.einsum('pqc,bq->pbc', first_cube.astype(jnp.float32), item_rows.astype(jnp.float32)).astype(jnp.bfloat16)
    second_flat = second.reshape(R1, BI * KC)
    predicted = jnp.dot(user_rows, second_flat, preferred_element_type=jnp.float32)
    residual = (predicted - observed_tile.reshape(BU, BI * KC).astype(jnp.float32)).astype(jnp.bfloat16)
    grad_user = jnp.dot(residual, second_flat.T, preferred_element_type=jnp.float32)
    back_flat = jnp.dot(user_rows.T, residual, preferred_element_type=jnp.float32).astype(jnp.bfloat16)
    back_cube = back_flat.reshape(R1, BI, KC)
    grad_item = jnp.einsum('pbc,pqc->bq', back_cube.astype(jnp.float32), first_cube.astype(jnp.float32))
    folded = jnp.einsum('pbc,bq->pqc', back_cube.astype(jnp.float32), item_rows.astype(jnp.float32)).astype(jnp.bfloat16)
    folded = folded.reshape(R1 * R2, KC)
    grad_ctx = jnp.dot(folded.T, core_half, preferred_element_type=jnp.float32)
    grad_core = jnp.dot(folded, ctx_rows, preferred_element_type=jnp.float32)
    return (grad_core, grad_user, grad_item, grad_ctx)

def reference(observed, user_block, item_block, stratum, context_ids, core_tensor, user_factor, item_factor, context_factor):
    core_half = core_tensor.astype(jnp.bfloat16)
    scale = 1.0 / math.sqrt(BU * BI * KC)
    tile_numbers = jnp.arange(TILES, dtype=jnp.int32)

    def step(carry, inputs):
        acc_core, acc_user, acc_item, acc_ctx = carry
        tile_data, ublock, iblock, item_shard, slice_ids, tile_number = inputs
        device = tile_number // TILES_DEV
        user_index = device // N_ITEM
        user_start = ((user_index * UB_DEV + ublock) * BU).astype(jnp.int32)
        item_start = ((item_shard * IB_DEV + iblock) * BI).astype(jnp.int32)
        user_rows = lax.dynamic_slice_in_dim(user_factor, user_start, BU, 0)
        item_rows = lax.dynamic_slice_in_dim(item_factor, item_start, BI, 0)
        ctx_rows = jnp.take(context_factor, slice_ids, axis=0)
        g_core, g_user, g_item, g_ctx = tile_terms(core_half, user_rows, item_rows, ctx_rows, tile_data)
        old_user = lax.dynamic_slice_in_dim(acc_user, user_start, BU, 0)
        acc_user = lax.dynamic_update_slice_in_dim(acc_user, old_user + g_user, user_start, 0)
        old_item = lax.dynamic_slice_in_dim(acc_item, item_start, BI, 0)
        acc_item = lax.dynamic_update_slice_in_dim(acc_item, old_item + g_item, item_start, 0)
        acc_ctx = acc_ctx.at[slice_ids].add(g_ctx)
        return ((acc_core + g_core, acc_user, acc_item, acc_ctx), None)
    init = (jnp.zeros((R1 * R2, R3), jnp.float32), jnp.zeros((NU, R1), jnp.float32), jnp.zeros((NI, R2), jnp.float32), jnp.zeros((NC, R3), jnp.float32))
    final, unused = lax.scan(step, init, (observed, user_block, item_block, stratum, context_ids, tile_numbers))
    acc_core, acc_user, acc_item, acc_ctx = final
    return (acc_core * scale, acc_user * scale, acc_item * scale, acc_ctx * scale)
```

```python
import functools
import math

import jax
import jax.numpy as jnp
from jax import lax
from jax.experimental import pallas as pl
from jax.experimental.pallas import tpu as pltpu
from jax.sharding import PartitionSpec as P

MESH = pl.DeviceIdType.MESH
F32 = jnp.float32
BF16 = jnp.bfloat16
VMEM_LIMIT = 56 * 1024 * 1024


def up16(rows):
    return (rows + 15) // 16 * 16


def dot(left, right, left_dim, right_dim):
    return lax.dot_general(
        left, right, (((left_dim,), (right_dim,)), ((), ())), preferred_element_type=F32
    )


class Grid:
    def __init__(self, users, items):
        nc = 2 if users % 2 == 0 else 1
        rest = users // nc
        ny = 1
        while rest % (2 * ny) == 0 and (2 * ny) * (2 * ny) <= rest:
            ny *= 2
        self.n = {"z": rest // ny, "y": ny, "c": nc, "x": items}

    def here(self):
        user = lax.axis_index("user")
        n = self.n
        return {
            "c": lax.rem(user, n["c"]),
            "y": lax.rem(lax.div(user, n["c"]), n["y"]),
            "z": lax.div(user, n["c"] * n["y"]),
            "x": lax.axis_index("item"),
        }

    def moved(self, at, **steps):
        out = dict(at)
        for axis, step in steps.items():
            if step:
                out[axis] = lax.rem(at[axis] + step + self.n[axis], self.n[axis])
        return out

    def device(self, at):
        n = self.n
        return ((at["z"] * n["y"] + at["y"]) * n["c"] + at["c"], at["x"])

    def shard(self, at):
        user, item = self.device(at)
        return user * self.n["x"] + item

    def partners(self, at):
        return [
            self.moved(at, **{axis: step})
            for axis in "zycx"
            for step in range(1, self.n[axis])
        ]


def enter(grid, at):
    barrier = pltpu.get_barrier_semaphore()
    others = grid.partners(at)
    for other in others:
        pl.semaphore_signal(barrier, inc=1, device_id=grid.device(other), device_id_type=MESH)
    pl.semaphore_wait(barrier, len(others))


class Wires:
    def __init__(self, grid, send_sems, recv_sems):
        self.grid, self.send, self.recv, self.used, self.copies = grid, send_sems, recv_sems, 0, []

    def start(self, src, dst, to):
        copy = pltpu.make_async_remote_copy(
            src_ref=src,
            dst_ref=dst,
            send_sem=self.send.at[self.used],
            recv_sem=self.recv.at[self.used],
            device_id=self.grid.device(to),
            device_id_type=MESH,
        )
        copy.start()
        self.used += 1
        self.copies.append(copy)
        return copy

    def finish(self):
        for copy in self.copies:
            copy.wait_send()


def halves(rows):
    first = up16(rows // 2)
    return (0, first), (first, rows - first)


def order(n):
    return [(step + 1) % n for step in range(n)]


def gather_kernel(grid, shard_ref, out_ref, send_sems, recv_sems):
    n = grid.n
    at = grid.here()
    rows = shard_ref.shape[0]
    out_ref[grid.shard(at)] = shard_ref[...]
    enter(grid, at)
    wires = Wires(grid, send_sems, recv_sems)

    def send(owner, part, **to):
        ref = out_ref.at[grid.shard(owner), pl.ds(*part)]
        return wires.start(ref, ref, grid.moved(at, **to))

    parts = [(part, *axes) for part, axes in zip(halves(rows), (("y", "x"), ("x", "y")))]
    first = {}
    for dz in range(1, n["z"]):
        for part, one, two in parts:
            first[dz, part] = send(at, part, z=dz)
    pending = []
    for dz in range(n["z"]):
        second = {}
        for part, one, two in parts:
            if dz:
                first[dz, part].wait_recv()
            mine = grid.moved(at, z=-dz)
            for d1 in range(1, n[one]):
                second[d1, part] = send(mine, part, **{one: d1})
        third = {}
        for part, one, two in parts:
            for d1 in range(n[one]):
                if d1:
                    second[d1, part].wait_recv()
                mine = grid.moved(at, **{"z": -dz, one: -d1})
                for d2 in range(1, n[two]):
                    third[d1, d2, part] = send(mine, part, **{two: d2})
        for part, one, two in parts:
            for d1 in range(n[one]):
                for d2 in range(n[two]):
                    if d2:
                        third[d1, d2, part].wait_recv()
                    mine = grid.moved(at, **{"z": -dz, one: -d1, two: -d2})
                    for dc in range(1, n["c"]):
                        pending.append(send(mine, part, c=dc))
    for copy in pending:
        copy.wait_recv()
    wires.finish()


def gather(grid, shard):
    n = grid.n
    total = n["z"] * n["y"] * n["c"] * n["x"]
    copies = 2 * (total - 1)
    return pl.pallas_call(
        functools.partial(gather_kernel, grid),
        out_shape=jax.ShapeDtypeStruct((total,) + shard.shape, shard.dtype),
        in_specs=[pl.BlockSpec(memory_space=pltpu.VMEM)],
        out_specs=pl.BlockSpec(memory_space=pltpu.VMEM),
        scratch_shapes=[pltpu.SemaphoreType.DMA((copies,)), pltpu.SemaphoreType.DMA((copies,))],
        compiler_params=pltpu.CompilerParams(
            collective_id=0, has_side_effects=True, vmem_limit_bytes=VMEM_LIMIT
        ),
        name="gather_factors",
    )(shard)


def tile_kernel(
    sizes, index_ref, ids_ref, observed_ref, all_ref, user_ref, terms_ref, user_out_ref,
    observed32_ref, first_ref, cube_ref,
):
    m, ni, nk, items, blocks, scale = sizes
    total, rows, _ = all_ref.shape
    bu, bi, kc = observed_ref.shape
    rank_two = kc_rank = all_ref.shape[2]
    rank_one = total * m // rank_two
    item_at, ctx_at = m, m + up16(ni)
    ctx_pad = rows - ctx_at
    user_block, item_block, stratum = index_ref[0], index_ref[1], index_ref[2]
    unit = max(m, 4 * rank_two)
    per, across = unit // m, unit // rank_two

    user_start = pl.multiple_of(user_block * bu, bu)
    user_rows = user_ref[pl.ds(user_start, bu), :]
    item_first = (item_block * (bi // ni)) * items + stratum
    item_rows = jnp.concatenate(
        [
            all_ref[item_first + j * items, pl.ds(item_at, up16(ni)), :].astype(F32)[:ni]
            for j in range(bi // ni)
        ],
        axis=0,
    ).astype(BF16)
    ids = ids_ref[...]
    places = lax.div(ids, jnp.full_like(ids, nk)) * ctx_pad + lax.rem(ids, jnp.full_like(ids, nk))
    spots = lax.broadcasted_iota(jnp.int32, (total * ctx_pad, kc), 0)
    picker = jnp.where(spots == places, 1.0, 0.0).astype(BF16)
    ctx_all = all_ref[:, pl.ds(ctx_at, ctx_pad), :].reshape(total * ctx_pad, kc_rank)
    ctx_rows = dot(picker, ctx_all, 0, 0).astype(BF16)

    def widen(a, carry):
        start = pl.multiple_of(a * bi, bi)
        observed32_ref[pl.ds(start, bi), :] = observed_ref[a].astype(F32)
        return carry

    lax.fori_loop(0, bu, widen, 0, unroll=4)

    def core_of(k):
        pieces = [all_ref[k * per + j, pl.ds(0, m), :] for j in range(per)]
        return pieces[0] if per == 1 else jnp.concatenate(pieces, axis=0)

    def forward(k, carry):
        first = dot(core_of(k), ctx_rows, 1, 1).astype(BF16)
        first_ref[pl.ds(pl.multiple_of(k * unit, unit), unit), :] = first
        wide = jnp.concatenate(
            [first[j * rank_two:(j + 1) * rank_two] for j in range(across)], axis=1
        )
        second = dot(item_rows, wide, 1, 0)
        for j in range(across):
            start = pl.multiple_of((k * across + j) * bi, bi)
            cube_ref[pl.ds(start, bi), :] = second[:, j * kc:(j + 1) * kc]
        return carry

    lax.fori_loop(0, total * m // unit, forward, 0)

    wide_b = 4

    def middle(k, grad_user):
        b = k * wide_b
        second = jnp.concatenate(
            [cube_ref[pl.ds(b + j, rank_one, stride=bi), :].astype(BF16) for j in range(wide_b)],
            axis=1,
        )
        seen = jnp.concatenate(
            [observed32_ref[pl.ds(b + j, bu, stride=bi), :] for j in range(wide_b)], axis=1
        )
        residual = (dot(user_rows, second, 1, 0) - seen).astype(BF16)
        back = dot(user_rows, residual, 0, 0)
        for j in range(wide_b):
            cube_ref[pl.ds(b + j, rank_one, stride=bi), :] = back[:, j * kc:(j + 1) * kc]
        return grad_user + dot(residual, second, 1, 1)

    grad_user = lax.fori_loop(0, bi // wide_b, middle, jnp.zeros((bu, rank_one), F32))
    user_out_ref[...] = jnp.zeros_like(user_out_ref)
    user_out_ref[pl.ds(user_start, bu), :] = grad_user * scale

    def backward(k, carry):
        grad_item, grad_ctx = carry
        start = pl.multiple_of(k * unit, unit)
        backs = [
            cube_ref[pl.ds(pl.multiple_of((k * across + j) * bi, bi), bi), :].astype(BF16)
            for j in range(across)
        ]
        firsts = [
            first_ref[pl.ds(pl.multiple_of(start + j * rank_two, rank_two), rank_two), :]
            for j in range(across)
        ]
        wide = jnp.concatenate(backs, axis=1)
        grad_item = grad_item + dot(wide, jnp.concatenate(firsts, axis=1), 1, 1)
        folded = dot(item_rows, wide, 0, 0).astype(BF16)
        folded = jnp.concatenate([folded[:, j * kc:(j + 1) * kc] for j in range(across)], axis=0)
        grad_ctx = grad_ctx + dot(folded, core_of(k), 0, 0)
        grad_core = (dot(folded, ctx_rows, 1, 0) * scale).astype(BF16)
        for j in range(per):
            terms_ref[k * per + j, pl.ds(0, m), :] = grad_core[j * m:(j + 1) * m]
        return grad_item, grad_ctx

    grad_item, grad_ctx = lax.fori_loop(
        0,
        total * m // unit,
        backward,
        (jnp.zeros((bi, rank_two), F32), jnp.zeros((kc, kc_rank), F32)),
    )
    terms_ref[:, pl.ds(item_at, up16(ni)), :] = jnp.zeros((total, up16(ni), rank_two), BF16)
    for j in range(bi // ni):
        piece = grad_item[j * ni:(j + 1) * ni] * scale
        if ni < up16(ni):
            piece = jnp.concatenate([piece, jnp.zeros((up16(ni) - ni, rank_two), F32)], axis=0)
        owner = (stratum * blocks + item_block) * (bi // ni) + j
        terms_ref[owner, pl.ds(item_at, up16(ni)), :] = piece.astype(BF16)
    grad_ctx = grad_ctx * scale
    high = grad_ctx.astype(BF16)
    low = (grad_ctx - high.astype(F32)).astype(BF16)
    spread = dot(picker, high, 1, 0) + dot(picker, low, 1, 0)
    terms_ref[:, pl.ds(ctx_at, ctx_pad), :] = spread.astype(BF16).reshape(total, ctx_pad, kc_rank)


def tile(sizes, index, ids, observed, everything, user_factor):
    bu, bi, kc = observed.shape
    total, rows, rank = everything.shape
    m = sizes[0]
    vmem = pl.BlockSpec(memory_space=pltpu.VMEM)
    cost = 9 * 2 * total * m * bi * kc
    return pl.pallas_call(
        functools.partial(tile_kernel, sizes),
        out_shape=(
            jax.ShapeDtypeStruct(everything.shape, BF16),
            jax.ShapeDtypeStruct(user_factor.shape, F32),
        ),
        in_specs=[pl.BlockSpec(memory_space=pltpu.SMEM)] + [vmem] * 4,
        out_specs=(vmem, vmem),
        scratch_shapes=[
            pltpu.VMEM((bu * bi, kc), F32),
            pltpu.VMEM((total * m, kc), BF16),
            pltpu.VMEM((total * m // rank * bi, kc), F32),
        ],
        compiler_params=pltpu.CompilerParams(vmem_limit_bytes=VMEM_LIMIT),
        cost_estimate=pl.CostEstimate(flops=cost, bytes_accessed=observed.size * 6, transcendentals=0),
        name="tile_gradients",
    )(index, ids, observed, everything, user_factor)


def scatter_kernel(
    grid, sizes, terms_ref, user_ref, core_out, item_out, ctx_out, user_out,
    c_in, keep, send_one, in_one, mid, send_two, in_two, send_three, in_three, user_in, total_ref,
    send_sems, recv_sems,
):
    m, ni, nk = sizes
    n = grid.n
    at = grid.here()
    rows = terms_ref.shape[1]
    enter(grid, at)
    wires = Wires(grid, send_sems, recv_sems)
    parts = [(part, *axes) for part, axes in zip(halves(rows), (("x", "y"), ("y", "x")))]
    both = n["x"] * n["y"]

    def spot(dx, dy):
        return dy * n["x"] + dx

    chunk = user_out.shape[0]
    user_copies = []
    for dx in range(1, n["x"]):
        to = grid.moved(at, x=dx)
        start = pl.multiple_of(to["x"] * chunk, chunk)
        user_copies.append(wires.start(user_ref.at[pl.ds(start, chunk)], user_in.at[dx - 1], to))

    zero = {}
    for dz in order(n["z"]):
        for dy in range(n["y"]):
            for dx in range(n["x"]):
                for dc in range(1, n["c"]):
                    to = grid.moved(at, z=dz, y=dy, x=dx, c=dc)
                    zero[dz, dy, dx, dc] = wires.start(
                        terms_ref.at[grid.shard(to)],
                        c_in.at[dc - 1, dz * both + spot(dx, dy)],
                        grid.moved(at, c=dc),
                    )
    one_copies, two_copies, three_copies = {}, {}, {}

    def stage_one(dz):
        for dy in range(n["y"]):
            for dx in range(n["x"]):
                for dc in range(1, n["c"]):
                    zero[dz, dy, dx, dc].wait_recv()
                own = grid.shard(grid.moved(at, z=dz, y=dy, x=dx))
                slot = dz * both + spot(dx, dy)
                for part, one, two in parts:
                    value = terms_ref[own, pl.ds(*part), :].astype(F32)
                    for dc in range(1, n["c"]):
                        value = value + c_in[dc - 1, slot, pl.ds(*part), :].astype(F32)
                    step = dx if one == "x" else dy
                    if not step:
                        keep[slot, pl.ds(*part), :] = value
                        continue
                    send_one[slot, pl.ds(*part), :] = value.astype(BF16)
                    one_copies[dz, dy, dx, part] = wires.start(
                        send_one.at[slot, pl.ds(*part)],
                        in_one.at[slot, pl.ds(*part)],
                        grid.moved(at, **{one: step}),
                    )

    def stage_two(dz):
        for part, one, two in parts:
            for d2 in range(n[two]):
                def steps(d1):
                    return (d1, d2) if one == "x" else (d2, d1)

                slot = dz * both + spot(*steps(0))
                value = keep[slot, pl.ds(*part), :]
                for d1 in range(1, n[one]):
                    dx, dy = steps(d1)
                    one_copies[dz, dy, dx, part].wait_recv()
                    value = value + in_one[dz * both + spot(dx, dy), pl.ds(*part), :].astype(F32)
                if not d2:
                    mid[dz, pl.ds(*part), :] = value
                    continue
                send_two[slot, pl.ds(*part), :] = value.astype(BF16)
                two_copies[dz, d2, part] = wires.start(
                    send_two.at[slot, pl.ds(*part)],
                    in_two.at[slot, pl.ds(*part)],
                    grid.moved(at, **{two: d2}),
                )

    def stage_three(dz):
        for part, one, two in parts:
            value = mid[dz, pl.ds(*part), :]
            for d2 in range(1, n[two]):
                dx, dy = (0, d2) if one == "x" else (d2, 0)
                two_copies[dz, d2, part].wait_recv()
                value = value + in_two[dz * both + spot(dx, dy), pl.ds(*part), :].astype(F32)
            if not dz:
                total_ref[pl.ds(*part), :] = value
                continue
            send_three[dz, pl.ds(*part), :] = value.astype(BF16)
            three_copies[dz, part] = wires.start(
                send_three.at[dz, pl.ds(*part)],
                in_three.at[dz, pl.ds(*part)],
                grid.moved(at, z=dz),
            )

    turns = order(n["z"])
    for k in range(len(turns) + 2):
        if k < len(turns):
            stage_one(turns[k])
        if 0 <= k - 1 < len(turns):
            stage_two(turns[k - 1])
        if 0 <= k - 2 < len(turns):
            stage_three(turns[k - 2])

    value = user_ref[pl.ds(pl.multiple_of(at["x"] * chunk, chunk), chunk), :]
    for dx, copy in enumerate(user_copies):
        copy.wait_recv()
        value = value + user_in[dx]
    user_out[...] = value
    for part, one, two in parts:
        value = total_ref[pl.ds(*part), :]
        for dz in range(1, n["z"]):
            three_copies[dz, part].wait_recv()
            value = value + in_three[dz, pl.ds(*part), :].astype(F32)
        total_ref[pl.ds(*part), :] = value
    core_out[...] = total_ref[pl.ds(0, m), :]
    item_out[...] = total_ref[pl.ds(m, ni), :]
    ctx_out[...] = total_ref[pl.ds(m + up16(ni), nk), :]
    wires.finish()


def scatter(grid, sizes, terms, term_user):
    m, ni, nk = sizes
    n = grid.n
    total, rows, rank = terms.shape
    chip = total // n["c"]
    chunk = term_user.shape[0] // n["x"]
    copies = 2 * total + n["x"]
    vmem = pl.BlockSpec(memory_space=pltpu.VMEM)
    plane = lambda count, kind: pltpu.VMEM((max(count, 1), rows, rank), kind)
    return pl.pallas_call(
        functools.partial(scatter_kernel, grid, sizes),
        out_shape=tuple(
            jax.ShapeDtypeStruct((count, rank), F32) for count in (m, ni, nk, chunk)
        ),
        in_specs=[vmem, vmem],
        out_specs=(vmem,) * 4,
        scratch_shapes=[
            pltpu.VMEM((max(n["c"] - 1, 1), chip, rows, rank), BF16),
            plane(chip, F32),
            plane(chip, BF16),
            plane(chip, BF16),
            plane(n["z"], F32),
            plane(chip, BF16),
            plane(chip, BF16),
            plane(n["z"], BF16),
            plane(n["z"], BF16),
            pltpu.VMEM((max(n["x"] - 1, 1), chunk, rank), F32),
            pltpu.VMEM((rows, rank), F32),
            pltpu.SemaphoreType.DMA((copies,)),
            pltpu.SemaphoreType.DMA((copies,)),
        ],
        compiler_params=pltpu.CompilerParams(
            collective_id=1, has_side_effects=True, vmem_limit_bytes=VMEM_LIMIT
        ),
        name="scatter_sums",
    )(terms, term_user)


def local(
    grid, observed, user_block, item_block, stratum, context_ids, core_tensor, user_factor,
    item_factor, context_factor,
):
    n = grid.n
    users, items = n["z"] * n["y"] * n["c"], n["x"]
    tiles_here, block_user, block_item, slices = observed.shape
    m = core_tensor.shape[0]
    ni = item_factor.shape[0] // users
    nk = context_factor.shape[0]
    rank = core_tensor.shape[1]
    scale = 1.0 / math.sqrt(block_user * block_item * slices)
    item_rows = lax.dynamic_slice_in_dim(item_factor, lax.axis_index("user") * ni, ni, 0)
    fill = lambda count: jnp.zeros((up16(count) - count, rank), BF16)
    shard = jnp.concatenate(
        [core_tensor.astype(BF16), item_rows, fill(ni), context_factor, fill(nk)], axis=0
    )
    everything = gather(grid, shard)
    sizes = (m, ni, nk, items, item_factor.shape[0] // block_item, scale)
    terms = term_user = None
    for t in range(tiles_here):
        index = jnp.stack([user_block[t], item_block[t], stratum[t]])
        one_terms, one_user = tile(
            sizes, index, context_ids[t:t + 1], observed[t], everything, user_factor
        )
        if t:
            terms = (terms.astype(F32) + one_terms.astype(F32)).astype(BF16)
            term_user = term_user + one_user
        else:
            terms, term_user = one_terms, one_user
    core_grad, item_grad, context_grad, user_grad = scatter(grid, (m, ni, nk), terms, term_user)
    return (core_grad, user_grad, item_grad, context_grad)


def solution(mesh):
    grid = Grid(mesh.shape["user"], mesh.shape["item"])
    both = ("user", "item")
    return jax.shard_map(
        functools.partial(local, grid),
        mesh=mesh,
        in_specs=(
            P(both, None, None, None),
            P(both),
            P(both),
            P(both),
            P(both, None),
            P(both, None),
            P("user", None),
            P("item", None),
            P(both, None),
        ),
        out_specs=(P(both, None), P(both, None), P(both, None), P(both, None)),
        check_vma=False,
    )
```

```python
import functools
import math

import jax
import jax.numpy as jnp
from jax import lax
from jax.experimental import pallas as pl
from jax.experimental.pallas import tpu as pltpu
from jax.sharding import PartitionSpec as P

MESH = pl.DeviceIdType.MESH
F32 = jnp.float32
BF16 = jnp.bfloat16
VMEM_LIMIT = 60 * 1024 * 1024


def up16(rows):
    return (rows + 15) // 16 * 16


def dot(left, right, left_dim, right_dim):
    return lax.dot_general(
        left, right, (((left_dim,), (right_dim,)), ((), ())), preferred_element_type=F32
    )


class Grid:
    def __init__(self, users, items):
        nc = 2 if users % 2 == 0 else 1
        rest = users // nc
        ny = 1
        while rest % (2 * ny) == 0 and (2 * ny) * (2 * ny) <= rest:
            ny *= 2
        self.n = {"z": rest // ny, "y": ny, "c": nc, "x": items}

    def here(self):
        user = lax.axis_index("user")
        n = self.n
        return {
            "c": lax.rem(user, n["c"]),
            "y": lax.rem(lax.div(user, n["c"]), n["y"]),
            "z": lax.div(user, n["c"] * n["y"]),
            "x": lax.axis_index("item"),
        }

    def moved(self, at, **steps):
        out = dict(at)
        for axis, step in steps.items():
            if step:
                out[axis] = lax.rem(at[axis] + step + self.n[axis], self.n[axis])
        return out

    def device(self, at):
        n = self.n
        return ((at["z"] * n["y"] + at["y"]) * n["c"] + at["c"], at["x"])

    def shard(self, at):
        user, item = self.device(at)
        return user * self.n["x"] + item

    def partners(self, at):
        return [
            self.moved(at, **{axis: step})
            for axis in "zycx"
            for step in range(1, self.n[axis])
        ]


def enter(grid, at):
    barrier = pltpu.get_barrier_semaphore()
    others = grid.partners(at)
    for other in others:
        pl.semaphore_signal(barrier, inc=1, device_id=grid.device(other), device_id_type=MESH)
    pl.semaphore_wait(barrier, len(others))


class Wires:
    def __init__(self, grid, send_sems, recv_sems):
        self.grid, self.send, self.recv, self.used, self.copies = grid, send_sems, recv_sems, 0, []

    def start(self, src, dst, to):
        copy = pltpu.make_async_remote_copy(
            src_ref=src,
            dst_ref=dst,
            send_sem=self.send.at[self.used],
            recv_sem=self.recv.at[self.used],
            device_id=self.grid.device(to),
            device_id_type=MESH,
        )
        copy.start()
        self.used += 1
        self.copies.append(copy)
        return copy

    def finish(self):
        for copy in self.copies:
            copy.wait_send()


def halves(rows):
    first = up16(rows // 2)
    return (0, first), (first, rows - first)


def order(n):
    return [(step + 1) % n for step in range(n)]


class GatherFlow:
    def __init__(self, wires, grid, at, ref, part, one, two):
        self.wires, self.grid, self.at, self.ref = wires, grid, at, ref
        self.part, self.one, self.two = part, one, two
        self.z, self.first, self.second, self.core = {}, {}, {}, {}

    def send(self, owner, **to):
        ref = self.ref.at[self.grid.shard(owner), pl.ds(*self.part)]
        return self.wires.start(ref, ref, self.grid.moved(self.at, **to))

    def start(self):
        for dz in range(1, self.grid.n["z"]):
            self.z[dz] = self.send(self.at, z=dz)

    def stage_one(self, dz):
        if dz:
            self.z[dz].wait_recv()
        owner = self.grid.moved(self.at, z=-dz)
        for d1 in range(1, self.grid.n[self.one]):
            self.first[dz, d1] = self.send(owner, **{self.one: d1})

    def stage_two(self, dz):
        for d1 in range(self.grid.n[self.one]):
            if d1:
                self.first[dz, d1].wait_recv()
            owner = self.grid.moved(self.at, **{"z": -dz, self.one: -d1})
            for d2 in range(1, self.grid.n[self.two]):
                self.second[dz, d1, d2] = self.send(owner, **{self.two: d2})

    def stage_core(self, dz):
        for d1 in range(self.grid.n[self.one]):
            for d2 in range(self.grid.n[self.two]):
                if d2:
                    self.second[dz, d1, d2].wait_recv()
                owner = self.grid.moved(self.at, **{"z": -dz, self.one: -d1, self.two: -d2})
                for dc in range(1, self.grid.n["c"]):
                    self.core[dz, d1, d2, dc] = self.send(owner, c=dc)

    def end(self, dz, dc):
        for key, copy in self.core.items():
            if key[0] == dz and key[3] == dc:
                copy.wait_recv()


class ScatterFlow:
    def __init__(self, wires, grid, at, terms, part, one, two, planes):
        self.wires, self.grid, self.at, self.terms = wires, grid, at, terms
        self.part, self.one, self.two, self.planes = part, one, two, planes
        self.core, self.first, self.second, self.z = {}, {}, {}, {}

    def rows(self):
        return pl.ds(*self.part)

    def slot(self, dz, d1, d2):
        n = self.grid.n
        return (dz * n[self.one] + d1) * n[self.two] + d2

    def send(self, name, target, slot, value, **to):
        rows = self.rows()
        self.planes["send_" + name][slot, rows, :] = value.astype(BF16)
        return self.wires.start(
            self.planes["send_" + name].at[slot, rows],
            self.planes["in_" + name].at[slot, rows],
            self.grid.moved(self.at, **to),
        )

    def got(self, name, slot):
        return self.planes["in_" + name][slot, self.rows(), :].astype(F32)

    def each(self):
        n = self.grid.n
        return [(d1, d2) for d1 in range(n[self.one]) for d2 in range(n[self.two])]

    def start(self, dz):
        chip = self.grid.n["z"] * len(self.each())
        for d1, d2 in self.each():
            for dc in range(1, self.grid.n["c"]):
                steps = {"z": dz, self.one: d1, self.two: d2, "c": dc}
                self.core[dz, d1, d2, dc] = self.wires.start(
                    self.terms.at[self.grid.shard(self.grid.moved(self.at, **steps)), self.rows()],
                    self.planes["in_c"].at[(dc - 1) * chip + self.slot(dz, d1, d2), self.rows()],
                    self.grid.moved(self.at, c=dc),
                )

    def stage_one(self, dz):
        chip = self.grid.n["z"] * len(self.each())
        for d1, d2 in reversed(self.each()):
            slot = self.slot(dz, d1, d2)
            own = self.grid.shard(self.grid.moved(self.at, **{"z": dz, self.one: d1, self.two: d2}))
            value = self.terms[own, self.rows(), :].astype(F32)
            for dc in range(1, self.grid.n["c"]):
                self.core[dz, d1, d2, dc].wait_recv()
                value = value + self.got("c", (dc - 1) * chip + slot)
            if d1:
                self.first[dz, d1, d2] = self.send("one", d1, slot, value, **{self.one: d1})
            else:
                self.planes["keep"][dz * self.grid.n[self.two] + d2, self.rows(), :] = value

    def stage_two(self, dz):
        for d2 in reversed(range(self.grid.n[self.two])):
            slot = dz * self.grid.n[self.two] + d2
            value = self.planes["keep"][slot, self.rows(), :]
            for d1 in range(1, self.grid.n[self.one]):
                self.first[dz, d1, d2].wait_recv()
                value = value + self.got("one", self.slot(dz, d1, d2))
            if d2:
                self.second[dz, d2] = self.send("two", d2, slot, value, **{self.two: d2})
            else:
                self.planes["mid"][dz, self.rows(), :] = value

    def stage_three(self, dz):
        value = self.planes["mid"][dz, self.rows(), :]
        for d2 in range(1, self.grid.n[self.two]):
            self.second[dz, d2].wait_recv()
            value = value + self.got("two", dz * self.grid.n[self.two] + d2)
        if dz:
            self.z[dz] = self.send("z", dz, dz, value, z=dz)
        else:
            self.planes["mid"][dz, self.rows(), :] = value

    def end(self):
        value = self.planes["mid"][0, self.rows(), :]
        for dz in range(1, self.grid.n["z"]):
            self.z[dz].wait_recv()
            value = value + self.got("z", dz)
        return value


PLANES = ("in_c", "keep", "send_one", "in_one", "mid", "send_two", "in_two", "send_z", "in_z")


def planes_for(grid, rows, rank):
    n = grid.n
    chip, most = n["z"] * n["y"] * n["x"], n["z"] * max(n["x"], n["y"])
    counts = {
        "in_c": chip * max(n["c"] - 1, 1),
        "send_one": chip,
        "in_one": chip,
        "keep": most,
        "send_two": most,
        "in_two": most,
        "mid": n["z"],
        "send_z": n["z"],
        "in_z": n["z"],
    }
    kind = lambda name: F32 if name in ("keep", "mid") else BF16
    return [pltpu.VMEM((counts[name], rows, rank), kind(name)) for name in PLANES]


def whole_kernel(
    grid, scale,
    user_block_ref, item_block_ref, stratum_ref, ids_ref, observed_hbm, core_ref, user_ref, item_ref,
    context_ref,
    core_out, item_out, ctx_out, user_out,
    observed_ref, wide_ref, item32_ref, cores_ref, first_ref, cube_ref, few_ref, few_terms_ref,
    user_terms_ref, user_in, *rest,
):
    count = len(PLANES)
    big = dict(zip(PLANES, rest[:count]))
    little = dict(zip(PLANES, rest[count:2 * count]))
    load_sem, send_sems, recv_sems = rest[2 * count:]
    n = grid.n
    at = grid.here()
    total, m, rank = cores_ref.shape
    bu, bi, kc = observed_ref.shape
    users = total // n["x"]
    ni, nk = item_ref.shape[0] // users, context_ref.shape[0]
    ni_pad, nk_pad = up16(ni), up16(nk)
    rank_two = rank
    rank_one = total * m // rank_two
    pitch = bi + 8
    group = n["x"] * m
    across = group // rank_two

    load = pltpu.make_async_copy(observed_hbm, observed_ref, load_sem)
    load.start()
    own = grid.shard(at)
    cores_ref[own] = core_ref[...].astype(BF16)
    item32_ref[...] = item_ref[...].astype(F32)
    start = pl.multiple_of(grid.device(at)[0] * ni, ni)

    def padded(value, rows):
        if value.shape[0] == rows:
            return value.astype(BF16)
        fill = jnp.zeros((rows - value.shape[0], rank), F32)
        return jnp.concatenate([value, fill], axis=0).astype(BF16)

    few_ref[own, pl.ds(0, ni_pad), :] = padded(item32_ref[pl.ds(start, ni), :], ni_pad)
    few_ref[own, pl.ds(ni_pad, nk_pad), :] = padded(context_ref[...].astype(F32), nk_pad)
    enter(grid, at)
    wires = Wires(grid, send_sems, recv_sems)
    low, high = halves(m)
    few_part = (0, ni_pad + nk_pad)
    few = GatherFlow(wires, grid, at, few_ref, few_part, "y", "x")
    flows = [
        GatherFlow(wires, grid, at, cores_ref, low, "y", "x"),
        GatherFlow(wires, grid, at, cores_ref, high, "x", "y"),
    ]
    few.start()
    few.stage_one(0)
    for flow in flows:
        flow.start()
    for flow in flows:
        flow.stage_one(0)
    for dz in range(1, n["z"]):
        few.stage_one(dz)
    load.wait()

    def widen(a, carry):
        row = pl.multiple_of(a * pitch, 8)
        wide_ref[pl.ds(row, bi), :] = observed_ref[a].astype(F32)
        return carry

    lax.fori_loop(0, bu, widen, 0, unroll=4)
    for dz in range(n["z"]):
        few.stage_two(dz)
    for flow in flows:
        flow.stage_two(0)
    for dz in range(n["z"]):
        few.stage_core(dz)
    if n["z"] > 1:
        for flow in flows:
            flow.stage_one(1)
    for dz in range(n["z"]):
        for dc in range(1, n["c"]):
            few.end(dz, dc)

    user_block, item_block, stratum = user_block_ref[0], item_block_ref[0], stratum_ref[0]
    blocks = item_ref.shape[0] // bi
    chosen = jnp.full((bu, rank), user_block, jnp.int32)
    user32 = jnp.zeros((bu, rank), F32)
    for j in range(user_ref.shape[0] // bu):
        user32 = jnp.where(chosen == j, user_ref[pl.ds(j * bu, bu), :].astype(F32), user32)
    user_rows, user_turned = user32.astype(BF16), user32.T.astype(BF16)
    chosen = jnp.full((bi, rank), stratum * blocks + item_block, jnp.int32)
    item32 = jnp.zeros((bi, rank), F32)
    for block in range(n["x"] * blocks):
        begin = (block % blocks) * (bi // ni) * n["x"] + block // blocks
        rows = jnp.concatenate(
            [
                few_ref[begin + j * n["x"], pl.ds(0, ni_pad), :].astype(F32)[:ni]
                for j in range(bi // ni)
            ],
            axis=0,
        )
        item32 = jnp.where(chosen == block, rows, item32)
    item_rows, item_turned = item32.astype(BF16), item32.T.astype(BF16)
    ids = ids_ref[...]
    places = lax.div(ids, jnp.full_like(ids, nk)) * nk_pad + lax.rem(ids, jnp.full_like(ids, nk))
    spots = lax.broadcasted_iota(jnp.int32, (total * nk_pad, kc), 0)
    picker = jnp.where(spots == places, 1.0, 0.0).astype(BF16)
    ctx_all = few_ref[:, pl.ds(ni_pad, nk_pad), :].reshape(total * nk_pad, rank)
    ctx32 = dot(picker, ctx_all, 0, 0)
    ctx_rows, ctx_turned = ctx32.astype(BF16), ctx32.T.astype(BF16)

    def first_shard(dz, dy, dc):
        z = lax.rem(at["z"] + dz + n["z"], n["z"])
        y = lax.rem(at["y"] + dy, n["y"])
        c = lax.rem(at["c"] + dc, n["c"])
        return ((z * n["y"] + y) * n["c"] + c) * n["x"]

    def forward(dz, dc):
        def step(dy, carry):
            shard = first_shard(-dz, dy, dc)
            core = cores_ref[pl.ds(shard, n["x"]), :, :].reshape(group, rank)
            first = dot(core, ctx_turned, 1, 0).astype(BF16)
            row = pl.multiple_of(shard * m, group)
            first_ref[pl.ds(row, group), :] = first
            wide = jnp.concatenate(
                [first[j * rank_two:(j + 1) * rank_two] for j in range(across)], axis=1
            )
            second = dot(item_rows, wide, 1, 0)
            p = lax.div(shard * m, rank_two)
            for j in range(across):
                cube_ref[pl.ds(pl.multiple_of((p + j) * pitch, 8), bi), :] = (
                    second[:, j * kc:(j + 1) * kc]
                )
            return carry

        lax.fori_loop(0, n["y"], step, 0)

    last = n["z"] - 1
    for k in range(n["z"] + 3):
        if 2 <= k <= last:
            for flow in flows:
                flow.stage_one(k)
        if 1 <= k - 1 <= last:
            for flow in flows:
                flow.stage_two(k - 1)
        if 0 <= k - 2 <= last:
            for flow in flows:
                flow.stage_core(k - 2)
            forward(k - 2, 0)
        if 0 <= k - 3 <= last:
            for dc in range(1, n["c"]):
                for flow in flows:
                    flow.end(k - 3, dc)
                forward(k - 3, dc)

    wide_b = 8

    def middle(k, grad_user):
        b = k * wide_b
        second = jnp.concatenate(
            [cube_ref[pl.ds(b + j, rank_one, stride=pitch), :].astype(BF16) for j in range(wide_b)],
            axis=1,
        )
        seen = jnp.concatenate(
            [wide_ref[pl.ds(b + j, bu, stride=pitch), :] for j in range(wide_b)], axis=1
        )
        residual = (dot(user_rows, second, 1, 0) - seen).astype(BF16)
        back = dot(user_turned, residual, 1, 0)
        for j in range(wide_b):
            cube_ref[pl.ds(b + j, rank_one, stride=pitch), :] = back[:, j * kc:(j + 1) * kc]
        return grad_user + dot(residual, second, 1, 1)

    grad_user = lax.fori_loop(0, bi // wide_b, middle, jnp.zeros((bu, rank_one), F32))
    grad_user = grad_user * scale
    for j in range(user_ref.shape[0] // bu):
        here = jnp.full(grad_user.shape, user_block, jnp.int32) == j
        user_terms_ref[pl.ds(j * bu, bu), :] = jnp.where(here, grad_user, 0.0)
    wires.finish()
    wires.copies = []

    chunk = user_out.shape[0]
    user_copies = []
    for dx in range(1, n["x"]):
        to = grid.moved(at, x=dx)
        start = pl.multiple_of(to["x"] * chunk, chunk)
        user_copies.append(
            wires.start(user_terms_ref.at[pl.ds(start, chunk)], user_in.at[dx - 1], to)
        )

    sums = [
        ScatterFlow(wires, grid, at, cores_ref, low, "x", "y", big),
        ScatterFlow(wires, grid, at, cores_ref, high, "y", "x", big),
    ]

    def backward(dz, dc, carry):
        def step(dy, carry):
            grad_item, grad_ctx = carry
            shard = first_shard(dz, dy, dc)
            p = lax.div(shard * m, rank_two)
            row = pl.multiple_of(shard * m, group)
            core = cores_ref[pl.ds(shard, n["x"]), :, :].reshape(group, rank)
            wide = jnp.concatenate(
                [
                    cube_ref[pl.ds(pl.multiple_of((p + j) * pitch, 8), bi), :].astype(BF16)
                    for j in range(across)
                ],
                axis=1,
            )
            first = first_ref[pl.ds(row, group), :]
            first = jnp.concatenate(
                [first[j * rank_two:(j + 1) * rank_two] for j in range(across)], axis=1
            )
            grad_item = grad_item + dot(wide, first, 1, 1)
            folded = dot(item_turned, wide, 1, 0).astype(BF16)
            folded = jnp.concatenate(
                [folded[:, j * kc:(j + 1) * kc] for j in range(across)], axis=0
            )
            grad_ctx = grad_ctx + dot(folded, core, 0, 0)
            grad_core = (dot(folded, ctx_rows, 1, 0) * scale).astype(BF16)
            cores_ref[pl.ds(shard, n["x"]), :, :] = grad_core.reshape(n["x"], m, rank)
            return grad_item, grad_ctx

        return lax.fori_loop(0, n["y"], step, carry)

    carry = (jnp.zeros((bi, rank_two), F32), jnp.zeros((kc, rank), F32))
    turns = order(n["z"])
    for k, dz in enumerate(turns):
        for dc in range(1, n["c"]):
            carry = backward(dz, dc, carry)
        for flow in sums:
            flow.start(dz)
        carry = backward(dz, 0, carry)
        if k + 1 < len(turns):
            for flow in sums:
                flow.stage_one(dz)
        if k >= 1:
            for flow in sums:
                flow.stage_two(turns[k - 1])
        if k >= 2:
            for flow in sums:
                flow.stage_three(turns[k - 2])

    grad_item, grad_ctx = carry
    grad_item, grad_ctx = grad_item * scale, grad_ctx * scale
    mine = jnp.full((ni_pad, rank), stratum * blocks + item_block, jnp.int32)
    for block in range(n["x"] * blocks):
        for j in range(bi // ni):
            piece = padded(grad_item[j * ni:(j + 1) * ni], ni_pad).astype(F32)
            few_terms_ref[block * (bi // ni) + j, pl.ds(0, ni_pad), :] = (
                jnp.where(mine == block, piece, 0.0).astype(BF16)
            )
    upper = grad_ctx.astype(BF16)
    lower = (grad_ctx - upper.astype(F32)).astype(BF16)
    spread = dot(picker, upper, 1, 0) + dot(picker, lower, 1, 0)
    few_terms_ref[:, pl.ds(ni_pad, nk_pad), :] = spread.astype(BF16).reshape(total, nk_pad, rank)
    few_sums = ScatterFlow(wires, grid, at, few_terms_ref, few_part, "x", "y", little)
    for dz in turns:
        few_sums.start(dz)
    for flow in sums:
        flow.stage_one(turns[-1])
    for dz in turns:
        few_sums.stage_one(dz)
    for flow in sums:
        flow.stage_two(turns[-1])
    if len(turns) >= 2:
        for flow in sums:
            flow.stage_three(turns[-2])
    for dz in turns:
        few_sums.stage_two(dz)
    for flow in sums:
        flow.stage_three(turns[-1])
    for dz in turns:
        few_sums.stage_three(dz)

    value = user_terms_ref[pl.ds(pl.multiple_of(at["x"] * chunk, chunk), chunk), :]
    for dx, copy in enumerate(user_copies):
        copy.wait_recv()
        value = value + user_in[dx]
    user_out[...] = value
    for flow in sums:
        core_out[pl.ds(*flow.part), :] = flow.end()
    value = few_sums.end()
    item_out[...] = value[:ni]
    ctx_out[...] = value[ni_pad:ni_pad + nk]
    wires.finish()


def whole(grid, scale, user_block, item_block, stratum, ids, observed, core, users, items, contexts):
    n = grid.n
    total = n["z"] * n["y"] * n["c"] * n["x"]
    bu, bi, kc = observed.shape
    m, rank = core.shape
    ni, nk = items.shape[0] // (total // n["x"]), contexts.shape[0]
    few = up16(ni) + up16(nk)
    chunk = users.shape[0] // n["x"]
    copies = 6 * total + n["x"]
    pitch = bi + 8
    vmem, smem = pl.BlockSpec(memory_space=pltpu.VMEM), pl.BlockSpec(memory_space=pltpu.SMEM)
    return pl.pallas_call(
        functools.partial(whole_kernel, grid, scale),
        out_shape=tuple(
            jax.ShapeDtypeStruct((count, rank), F32) for count in (m, ni, nk, chunk)
        ),
        in_specs=[smem] * 3 + [vmem, pl.BlockSpec(memory_space=pl.ANY)] + [vmem] * 4,
        out_specs=(vmem,) * 4,
        scratch_shapes=[
            pltpu.VMEM((bu, bi, kc), BF16),
            pltpu.VMEM((bu * pitch, kc), F32),
            pltpu.VMEM(items.shape, F32),
            pltpu.VMEM((total, m, rank), BF16),
            pltpu.VMEM((total * m, kc), BF16),
            pltpu.VMEM((total * m // rank * pitch, kc), F32),
            pltpu.VMEM((total, few, rank), BF16),
            pltpu.VMEM((total, few, rank), BF16),
            pltpu.VMEM(users.shape, F32),
            pltpu.VMEM((max(n["x"] - 1, 1), chunk, rank), F32),
            *planes_for(grid, m, rank),
            *planes_for(grid, few, rank),
            pltpu.SemaphoreType.DMA,
            pltpu.SemaphoreType.DMA((copies,)),
            pltpu.SemaphoreType.DMA((copies,)),
        ],
        compiler_params=pltpu.CompilerParams(
            collective_id=0, has_side_effects=True, vmem_limit_bytes=VMEM_LIMIT
        ),
        cost_estimate=pl.CostEstimate(
            flops=9 * 2 * total * m * bi * kc, bytes_accessed=observed.size * 2, transcendentals=0
        ),
        name="tucker_gradient",
    )(user_block, item_block, stratum, ids, observed, core, users, items, contexts)


def hand_over_kernel(*refs):
    half = len(refs) // 2
    for source, target in zip(refs[:half], refs[half:]):
        target[...] = source[...]


def hand_over(arrays):
    vmem = pl.BlockSpec(memory_space=pltpu.VMEM)
    return pl.pallas_call(
        hand_over_kernel,
        out_shape=tuple(jax.ShapeDtypeStruct(a.shape, a.dtype) for a in arrays),
        in_specs=[vmem] * len(arrays),
        out_specs=(vmem,) * len(arrays),
        name="hand_over",
    )(*arrays)


def local(
    grid, observed, user_block, item_block, stratum, context_ids, core_tensor, user_factor,
    item_factor, context_factor,
):
    tiles_here, block_user, block_item, slices = observed.shape
    scale = 1.0 / math.sqrt(block_user * block_item * slices)
    sums = None
    for t in range(tiles_here):
        one = slice(t, t + 1)
        terms = whole(
            grid, scale, user_block[one], item_block[one], stratum[one], context_ids[one],
            observed[t], core_tensor, user_factor, item_factor, context_factor,
        )
        sums = terms if sums is None else tuple(a + b for a, b in zip(sums, terms))
    core_grad, item_grad, context_grad, user_grad = hand_over(sums)
    return (core_grad, user_grad, item_grad, context_grad)


def solution(mesh):
    grid = Grid(mesh.shape["user"], mesh.shape["item"])
    both = ("user", "item")
    return jax.shard_map(
        functools.partial(local, grid),
        mesh=mesh,
        in_specs=(
            P(both, None, None, None),
            P(both),
            P(both),
            P(both),
            P(both, None),
            P(both, None),
            P("user", None),
            P("item", None),
            P(both, None),
        ),
        out_specs=(P(both, None), P(both, None), P(both, None), P(both, None)),
        check_vma=False,
    )
```

```python
import functools
import math

import jax
import jax.numpy as jnp
from jax import lax
from jax.experimental import pallas as pl
from jax.experimental.pallas import tpu as pltpu
from jax.sharding import PartitionSpec as P

MESH = pl.DeviceIdType.MESH
F32 = jnp.float32
BF16 = jnp.bfloat16
VMEM_LIMIT = 60 * 1024 * 1024


def up16(rows):
    return (rows + 15) // 16 * 16


def dot(left, right, left_dim, right_dim):
    return lax.dot_general(
        left, right, (((left_dim,), (right_dim,)), ((), ())), preferred_element_type=F32
    )


class Grid:
    def __init__(self, users, items):
        nc = 2 if users % 2 == 0 else 1
        rest = users // nc
        ny = 1
        while rest % (2 * ny) == 0 and (2 * ny) * (2 * ny) <= rest:
            ny *= 2
        self.n = {"z": rest // ny, "y": ny, "c": nc, "x": items}

    def here(self):
        user = lax.axis_index("user")
        n = self.n
        return {
            "c": lax.rem(user, n["c"]),
            "y": lax.rem(lax.div(user, n["c"]), n["y"]),
            "z": lax.div(user, n["c"] * n["y"]),
            "x": lax.axis_index("item"),
        }

    def moved(self, at, **steps):
        out = dict(at)
        for axis, step in steps.items():
            if step:
                out[axis] = lax.rem(at[axis] + step + self.n[axis], self.n[axis])
        return out

    def device(self, at):
        n = self.n
        return ((at["z"] * n["y"] + at["y"]) * n["c"] + at["c"], at["x"])

    def shard(self, at):
        user, item = self.device(at)
        return user * self.n["x"] + item

    def partners(self, at):
        return [
            self.moved(at, **{axis: step})
            for axis in "zycx"
            for step in range(1, self.n[axis])
        ]


def enter(grid, at):
    barrier = pltpu.get_barrier_semaphore()
    others = grid.partners(at)
    for other in others:
        pl.semaphore_signal(barrier, inc=1, device_id=grid.device(other), device_id_type=MESH)
    pl.semaphore_wait(barrier, len(others))


class Wires:
    def __init__(self, grid, send_sems, recv_sems):
        self.grid, self.send, self.recv, self.used, self.copies = grid, send_sems, recv_sems, 0, []

    def start(self, src, dst, to):
        copy = pltpu.make_async_remote_copy(
            src_ref=src,
            dst_ref=dst,
            send_sem=self.send.at[self.used],
            recv_sem=self.recv.at[self.used],
            device_id=self.grid.device(to),
            device_id_type=MESH,
        )
        copy.start()
        self.used += 1
        self.copies.append(copy)
        return copy

    def finish(self):
        for copy in self.copies:
            copy.wait_send()


def halves(rows):
    first = up16(rows // 2)
    return (0, first), (first, rows - first)


def order(n):
    return [(step + 1) % n for step in range(n)]


class GatherFlow:
    def __init__(self, wires, grid, at, ref, part, one, two):
        self.wires, self.grid, self.at, self.ref = wires, grid, at, ref
        self.part, self.one, self.two = part, one, two
        self.z, self.first, self.second, self.core = {}, {}, {}, {}

    def send(self, owner, **to):
        ref = self.ref.at[self.grid.shard(owner), pl.ds(*self.part)]
        return self.wires.start(ref, ref, self.grid.moved(self.at, **to))

    def start(self):
        for dz in range(1, self.grid.n["z"]):
            self.z[dz] = self.send(self.at, z=dz)

    def stage_one(self, dz):
        if dz:
            self.z[dz].wait_recv()
        owner = self.grid.moved(self.at, z=-dz)
        for d1 in range(1, self.grid.n[self.one]):
            self.first[dz, d1] = self.send(owner, **{self.one: d1})

    def stage_two(self, dz):
        for d1 in range(self.grid.n[self.one]):
            if d1:
                self.first[dz, d1].wait_recv()
            owner = self.grid.moved(self.at, **{"z": -dz, self.one: -d1})
            for d2 in range(1, self.grid.n[self.two]):
                self.second[dz, d1, d2] = self.send(owner, **{self.two: d2})

    def stage_core(self, dz):
        for d1 in range(self.grid.n[self.one]):
            for d2 in range(self.grid.n[self.two]):
                if d2:
                    self.second[dz, d1, d2].wait_recv()
                owner = self.grid.moved(self.at, **{"z": -dz, self.one: -d1, self.two: -d2})
                for dc in range(1, self.grid.n["c"]):
                    self.core[dz, d1, d2, dc] = self.send(owner, c=dc)

    def end(self, dz, dc):
        for key, copy in self.core.items():
            if key[0] == dz and key[3] == dc:
                copy.wait_recv()


class ScatterFlow:
    def __init__(self, wires, grid, at, terms, part, one, two, planes):
        self.wires, self.grid, self.at, self.terms = wires, grid, at, terms
        self.part, self.one, self.two, self.planes = part, one, two, planes
        self.core, self.first, self.second, self.z = {}, {}, {}, {}

    def rows(self):
        return pl.ds(*self.part)

    def slot(self, dz, d1, d2):
        n = self.grid.n
        return (dz * n[self.one] + d1) * n[self.two] + d2

    def send(self, name, target, slot, value, **to):
        rows = self.rows()
        self.planes["send_" + name][slot, rows, :] = value.astype(BF16)
        return self.wires.start(
            self.planes["send_" + name].at[slot, rows],
            self.planes["in_" + name].at[slot, rows],
            self.grid.moved(self.at, **to),
        )

    def got(self, name, slot):
        return self.planes["in_" + name][slot, self.rows(), :].astype(F32)

    def each(self):
        n = self.grid.n
        return [(d1, d2) for d1 in range(n[self.one]) for d2 in range(n[self.two])]

    def start(self, dz):
        chip = self.grid.n["z"] * len(self.each())
        for d1, d2 in self.each():
            for dc in range(1, self.grid.n["c"]):
                steps = {"z": dz, self.one: d1, self.two: d2, "c": dc}
                self.core[dz, d1, d2, dc] = self.wires.start(
                    self.terms.at[self.grid.shard(self.grid.moved(self.at, **steps)), self.rows()],
                    self.planes["in_c"].at[(dc - 1) * chip + self.slot(dz, d1, d2), self.rows()],
                    self.grid.moved(self.at, c=dc),
                )

    def stage_one(self, dz):
        chip = self.grid.n["z"] * len(self.each())
        for d1, d2 in reversed(self.each()):
            slot = self.slot(dz, d1, d2)
            own = self.grid.shard(self.grid.moved(self.at, **{"z": dz, self.one: d1, self.two: d2}))
            value = self.terms[own, self.rows(), :].astype(F32)
            for dc in range(1, self.grid.n["c"]):
                self.core[dz, d1, d2, dc].wait_recv()
                value = value + self.got("c", (dc - 1) * chip + slot)
            if d1:
                self.first[dz, d1, d2] = self.send("one", d1, slot, value, **{self.one: d1})
            else:
                self.planes["keep"][dz * self.grid.n[self.two] + d2, self.rows(), :] = value

    def stage_two(self, dz):
        for d2 in reversed(range(self.grid.n[self.two])):
            slot = dz * self.grid.n[self.two] + d2
            value = self.planes["keep"][slot, self.rows(), :]
            for d1 in range(1, self.grid.n[self.one]):
                self.first[dz, d1, d2].wait_recv()
                value = value + self.got("one", self.slot(dz, d1, d2))
            if d2:
                self.second[dz, d2] = self.send("two", d2, slot, value, **{self.two: d2})
            else:
                self.planes["mid"][dz, self.rows(), :] = value

    def stage_three(self, dz):
        value = self.planes["mid"][dz, self.rows(), :]
        for d2 in range(1, self.grid.n[self.two]):
            self.second[dz, d2].wait_recv()
            value = value + self.got("two", dz * self.grid.n[self.two] + d2)
        if dz:
            self.z[dz] = self.send("z", dz, dz, value, z=dz)
        else:
            self.planes["mid"][dz, self.rows(), :] = value

    def end(self):
        value = self.planes["mid"][0, self.rows(), :]
        for dz in range(1, self.grid.n["z"]):
            self.z[dz].wait_recv()
            value = value + self.got("z", dz)
        return value


PLANES = ("in_c", "keep", "send_one", "in_one", "mid", "send_two", "in_two", "send_z", "in_z")


def planes_for(grid, rows, rank):
    n = grid.n
    chip, most = n["z"] * n["y"] * n["x"], n["z"] * max(n["x"], n["y"])
    counts = {
        "in_c": chip * max(n["c"] - 1, 1),
        "send_one": chip,
        "in_one": chip,
        "keep": most,
        "send_two": most,
        "in_two": most,
        "mid": n["z"],
        "send_z": n["z"],
        "in_z": n["z"],
    }
    kind = lambda name: F32 if name in ("keep", "mid") else BF16
    return [pltpu.VMEM((counts[name], rows, rank), kind(name)) for name in PLANES]


def whole_kernel(
    grid, scale,
    user_block_ref, item_block_ref, stratum_ref, ids_ref, observed_hbm, core_ref, user_ref, item_ref,
    context_ref,
    core_out, item_out, ctx_out, user_out,
    observed_ref, wide_ref, item32_ref, cores_ref, first_ref, cube_ref, few_ref, few_terms_ref,
    user_terms_ref, user_in, *rest,
):
    count = len(PLANES)
    big = dict(zip(PLANES, rest[:count]))
    little = dict(zip(PLANES, rest[count:2 * count]))
    load_sem, send_sems, recv_sems = rest[2 * count:]
    n = grid.n
    at = grid.here()
    total, m, rank = cores_ref.shape
    bu, bi, kc = observed_ref.shape
    users = total // n["x"]
    ni, nk = item_ref.shape[0] // users, context_ref.shape[0]
    ni_pad, nk_pad = up16(ni), up16(nk)
    rank_two = rank
    rank_one = total * m // rank_two
    pitch = bi + 8
    group = n["x"] * m
    across = group // rank_two

    load = pltpu.make_async_copy(observed_hbm, observed_ref, load_sem)
    load.start()
    own = grid.shard(at)
    cores_ref[own] = core_ref[...].astype(BF16)
    item32_ref[...] = item_ref[...].astype(F32)
    start = pl.multiple_of(grid.device(at)[0] * ni, ni)

    def padded(value, rows):
        if value.shape[0] == rows:
            return value.astype(BF16)
        fill = jnp.zeros((rows - value.shape[0], rank), F32)
        return jnp.concatenate([value, fill], axis=0).astype(BF16)

    few_ref[own, pl.ds(0, ni_pad), :] = padded(item32_ref[pl.ds(start, ni), :], ni_pad)
    few_ref[own, pl.ds(ni_pad, nk_pad), :] = padded(context_ref[...].astype(F32), nk_pad)
    enter(grid, at)
    wires = Wires(grid, send_sems, recv_sems)
    low, high = halves(m)
    few_part = (0, ni_pad + nk_pad)
    few = GatherFlow(wires, grid, at, few_ref, few_part, "y", "x")
    flows = [
        GatherFlow(wires, grid, at, cores_ref, low, "y", "x"),
        GatherFlow(wires, grid, at, cores_ref, high, "x", "y"),
    ]
    last = n["z"] - 1

    def each(stage, dz):
        if dz <= last:
            for flow in flows:
                getattr(flow, stage)(dz)

    few.start()
    few.stage_one(0)
    for flow in flows:
        flow.start()
    each("stage_one", 0)
    for dz in range(1, n["z"]):
        few.stage_one(dz)
    each("stage_two", 0)
    for dz in range(n["z"]):
        few.stage_two(dz)
    each("stage_one", 1)
    for dz in range(n["z"]):
        few.stage_core(dz)
    each("stage_core", 0)
    each("stage_two", 1)
    load.wait()

    def widen(quarter):
        def step(a, carry):
            row = pl.multiple_of(a * pitch, 8)
            wide_ref[pl.ds(row, bi), :] = observed_ref[a].astype(F32)
            return carry

        lax.fori_loop(bu * quarter // n["z"], bu * (quarter + 1) // n["z"], step, 0, unroll=4)

    widen(0)
    for dz in range(n["z"]):
        for dc in range(1, n["c"]):
            few.end(dz, dc)

    user_block, item_block, stratum = user_block_ref[0], item_block_ref[0], stratum_ref[0]
    blocks = item_ref.shape[0] // bi
    chosen = jnp.full((bu, rank), user_block, jnp.int32)
    user32 = jnp.zeros((bu, rank), F32)
    for j in range(user_ref.shape[0] // bu):
        user32 = jnp.where(chosen == j, user_ref[pl.ds(j * bu, bu), :].astype(F32), user32)
    user_rows, user_turned = user32.astype(BF16), user32.T.astype(BF16)
    chosen = jnp.full((bi, rank), stratum * blocks + item_block, jnp.int32)
    item32 = jnp.zeros((bi, rank), F32)
    for block in range(n["x"] * blocks):
        begin = (block % blocks) * (bi // ni) * n["x"] + block // blocks
        rows = jnp.concatenate(
            [
                few_ref[begin + j * n["x"], pl.ds(0, ni_pad), :].astype(F32)[:ni]
                for j in range(bi // ni)
            ],
            axis=0,
        )
        item32 = jnp.where(chosen == block, rows, item32)
    item_rows, item_turned = item32.astype(BF16), item32.T.astype(BF16)
    ids = ids_ref[...]
    places = lax.div(ids, jnp.full_like(ids, nk)) * nk_pad + lax.rem(ids, jnp.full_like(ids, nk))
    spots = lax.broadcasted_iota(jnp.int32, (total * nk_pad, kc), 0)
    picker = jnp.where(spots == places, 1.0, 0.0).astype(BF16)
    ctx_all = few_ref[:, pl.ds(ni_pad, nk_pad), :].reshape(total * nk_pad, rank)
    ctx32 = dot(picker, ctx_all, 0, 0)
    ctx_rows, ctx_turned = ctx32.astype(BF16), ctx32.T.astype(BF16)

    def first_shard(dz, dy, dc):
        z = lax.rem(at["z"] + dz + n["z"], n["z"])
        y = lax.rem(at["y"] + dy, n["y"])
        c = lax.rem(at["c"] + dc, n["c"])
        return ((z * n["y"] + y) * n["c"] + c) * n["x"]

    def forward(dz, dc):
        def step(dy, carry):
            shard = first_shard(-dz, dy, dc)
            core = cores_ref[pl.ds(shard, n["x"]), :, :].reshape(group, rank)
            first = dot(core, ctx_turned, 1, 0).astype(BF16)
            row = pl.multiple_of(shard * m, group)
            first_ref[pl.ds(row, group), :] = first
            wide = jnp.concatenate(
                [first[j * rank_two:(j + 1) * rank_two] for j in range(across)], axis=1
            )
            second = dot(item_rows, wide, 1, 0)
            p = lax.div(shard * m, rank_two)
            for j in range(across):
                cube_ref[pl.ds(pl.multiple_of((p + j) * pitch, 8), bi), :] = (
                    second[:, j * kc:(j + 1) * kc]
                )
            return carry

        lax.fori_loop(0, n["y"], step, 0)

    for k in range(2, n["z"] + 2):
        each("stage_one", k)
        forward(k - 2, 0)
        each("stage_two", k)
        each("stage_core", k - 1)
        if k - 1 <= last:
            widen(k - 1)
        for dc in range(1, n["c"]):
            for flow in flows:
                flow.end(k - 2, dc)
            forward(k - 2, dc)

    wide_b = 8

    def middle(k, grad_user):
        b = k * wide_b
        second = jnp.concatenate(
            [cube_ref[pl.ds(b + j, rank_one, stride=pitch), :].astype(BF16) for j in range(wide_b)],
            axis=1,
        )
        seen = jnp.concatenate(
            [wide_ref[pl.ds(b + j, bu, stride=pitch), :] for j in range(wide_b)], axis=1
        )
        residual = (dot(user_rows, second, 1, 0) - seen).astype(BF16)
        back = dot(user_turned, residual, 1, 0)
        for j in range(wide_b):
            cube_ref[pl.ds(b + j, rank_one, stride=pitch), :] = back[:, j * kc:(j + 1) * kc]
        return grad_user + dot(residual, second, 1, 1)

    grad_user = lax.fori_loop(0, bi // wide_b, middle, jnp.zeros((bu, rank_one), F32))
    grad_user = grad_user * scale
    for j in range(user_ref.shape[0] // bu):
        here = jnp.full(grad_user.shape, user_block, jnp.int32) == j
        user_terms_ref[pl.ds(j * bu, bu), :] = jnp.where(here, grad_user, 0.0)
    wires.finish()
    wires.copies = []

    chunk = user_out.shape[0]
    user_copies = []
    for dx in range(1, n["x"]):
        to = grid.moved(at, x=dx)
        start = pl.multiple_of(to["x"] * chunk, chunk)
        user_copies.append(
            wires.start(user_terms_ref.at[pl.ds(start, chunk)], user_in.at[dx - 1], to)
        )

    sums = [
        ScatterFlow(wires, grid, at, cores_ref, low, "x", "y", big),
        ScatterFlow(wires, grid, at, cores_ref, high, "y", "x", big),
    ]

    def backward(dz, dc, carry):
        def step(dy, carry):
            grad_item, grad_ctx = carry
            shard = first_shard(dz, dy, dc)
            p = lax.div(shard * m, rank_two)
            row = pl.multiple_of(shard * m, group)
            core = cores_ref[pl.ds(shard, n["x"]), :, :].reshape(group, rank)
            wide = jnp.concatenate(
                [
                    cube_ref[pl.ds(pl.multiple_of((p + j) * pitch, 8), bi), :].astype(BF16)
                    for j in range(across)
                ],
                axis=1,
            )
            first = first_ref[pl.ds(row, group), :]
            first = jnp.concatenate(
                [first[j * rank_two:(j + 1) * rank_two] for j in range(across)], axis=1
            )
            grad_item = grad_item + dot(wide, first, 1, 1)
            folded = dot(item_turned, wide, 1, 0).astype(BF16)
            folded = jnp.concatenate(
                [folded[:, j * kc:(j + 1) * kc] for j in range(across)], axis=0
            )
            grad_ctx = grad_ctx + dot(folded, core, 0, 0)
            grad_core = (dot(folded, ctx_rows, 1, 0) * scale).astype(BF16)
            cores_ref[pl.ds(shard, n["x"]), :, :] = grad_core.reshape(n["x"], m, rank)
            return grad_item, grad_ctx

        return lax.fori_loop(0, n["y"], step, carry)

    carry = (jnp.zeros((bi, rank_two), F32), jnp.zeros((kc, rank), F32))
    turns = order(n["z"])
    for k, dz in enumerate(turns):
        for dc in range(1, n["c"]):
            carry = backward(dz, dc, carry)
        for flow in sums:
            flow.start(dz)
        if k >= 1:
            for flow in sums:
                flow.stage_two(turns[k - 1])
        carry = backward(dz, 0, carry)
        for flow in sums:
            flow.stage_one(dz)
        if k >= 1:
            for flow in sums:
                flow.stage_three(turns[k - 1])

    grad_item, grad_ctx = carry
    grad_item, grad_ctx = grad_item * scale, grad_ctx * scale
    mine = jnp.full((ni_pad, rank), stratum * blocks + item_block, jnp.int32)
    for block in range(n["x"] * blocks):
        for j in range(bi // ni):
            piece = padded(grad_item[j * ni:(j + 1) * ni], ni_pad).astype(F32)
            few_terms_ref[block * (bi // ni) + j, pl.ds(0, ni_pad), :] = (
                jnp.where(mine == block, piece, 0.0).astype(BF16)
            )
    upper = grad_ctx.astype(BF16)
    lower = (grad_ctx - upper.astype(F32)).astype(BF16)
    spread = dot(picker, upper, 1, 0) + dot(picker, lower, 1, 0)
    few_terms_ref[:, pl.ds(ni_pad, nk_pad), :] = spread.astype(BF16).reshape(total, nk_pad, rank)
    few_sums = ScatterFlow(wires, grid, at, few_terms_ref, few_part, "x", "y", little)
    for dz in turns:
        few_sums.start(dz)
    for flow in sums:
        flow.stage_two(turns[-1])
    for dz in turns:
        few_sums.stage_one(dz)
    for flow in sums:
        flow.stage_three(turns[-1])
    for dz in turns:
        few_sums.stage_two(dz)
    for dz in turns:
        few_sums.stage_three(dz)

    value = user_terms_ref[pl.ds(pl.multiple_of(at["x"] * chunk, chunk), chunk), :]
    for dx, copy in enumerate(user_copies):
        copy.wait_recv()
        value = value + user_in[dx]
    user_out[...] = value
    for flow in sums:
        core_out[pl.ds(*flow.part), :] = flow.end()
    value = few_sums.end()
    item_out[...] = value[:ni]
    ctx_out[...] = value[ni_pad:ni_pad + nk]
    wires.finish()


def whole(grid, scale, user_block, item_block, stratum, ids, observed, core, users, items, contexts):
    n = grid.n
    total = n["z"] * n["y"] * n["c"] * n["x"]
    bu, bi, kc = observed.shape
    m, rank = core.shape
    ni, nk = items.shape[0] // (total // n["x"]), contexts.shape[0]
    few = up16(ni) + up16(nk)
    chunk = users.shape[0] // n["x"]
    copies = 6 * total + n["x"]
    pitch = bi + 8
    vmem, smem = pl.BlockSpec(memory_space=pltpu.VMEM), pl.BlockSpec(memory_space=pltpu.SMEM)
    return pl.pallas_call(
        functools.partial(whole_kernel, grid, scale),
        out_shape=tuple(
            jax.ShapeDtypeStruct((count, rank), F32) for count in (m, ni, nk, chunk)
        ),
        in_specs=[smem] * 3 + [vmem, pl.BlockSpec(memory_space=pl.ANY)] + [vmem] * 4,
        out_specs=(vmem,) * 4,
        scratch_shapes=[
            pltpu.VMEM((bu, bi, kc), BF16),
            pltpu.VMEM((bu * pitch, kc), F32),
            pltpu.VMEM(items.shape, F32),
            pltpu.VMEM((total, m, rank), BF16),
            pltpu.VMEM((total * m, kc), BF16),
            pltpu.VMEM((total * m // rank * pitch, kc), F32),
            pltpu.VMEM((total, few, rank), BF16),
            pltpu.VMEM((total, few, rank), BF16),
            pltpu.VMEM(users.shape, F32),
            pltpu.VMEM((max(n["x"] - 1, 1), chunk, rank), F32),
            *planes_for(grid, m, rank),
            *planes_for(grid, few, rank),
            pltpu.SemaphoreType.DMA,
            pltpu.SemaphoreType.DMA((copies,)),
            pltpu.SemaphoreType.DMA((copies,)),
        ],
        compiler_params=pltpu.CompilerParams(
            collective_id=0, has_side_effects=True, vmem_limit_bytes=VMEM_LIMIT
        ),
        cost_estimate=pl.CostEstimate(
            flops=9 * 2 * total * m * bi * kc, bytes_accessed=observed.size * 2, transcendentals=0
        ),
        name="tucker_gradient",
    )(user_block, item_block, stratum, ids, observed, core, users, items, contexts)


def hand_over_kernel(*refs):
    half = len(refs) // 2
    for source, target in zip(refs[:half], refs[half:]):
        target[...] = source[...]


def hand_over(arrays):
    vmem = pl.BlockSpec(memory_space=pltpu.VMEM)
    return pl.pallas_call(
        hand_over_kernel,
        out_shape=tuple(jax.ShapeDtypeStruct(a.shape, a.dtype) for a in arrays),
        in_specs=[vmem] * len(arrays),
        out_specs=(vmem,) * len(arrays),
        name="hand_over",
    )(*arrays)


def local(
    grid, observed, user_block, item_block, stratum, context_ids, core_tensor, user_factor,
    item_factor, context_factor,
):
    tiles_here, block_user, block_item, slices = observed.shape
    scale = 1.0 / math.sqrt(block_user * block_item * slices)
    sums = None
    for t in range(tiles_here):
        one = slice(t, t + 1)
        terms = whole(
            grid, scale, user_block[one], item_block[one], stratum[one], context_ids[one],
            observed[t], core_tensor, user_factor, item_factor, context_factor,
        )
        sums = terms if sums is None else tuple(a + b for a, b in zip(sums, terms))
    core_grad, item_grad, context_grad, user_grad = hand_over(sums)
    return (core_grad, user_grad, item_grad, context_grad)


def solution(mesh):
    grid = Grid(mesh.shape["user"], mesh.shape["item"])
    both = ("user", "item")
    return jax.shard_map(
        functools.partial(local, grid),
        mesh=mesh,
        in_specs=(
            P(both, None, None, None),
            P(both),
            P(both),
            P(both),
            P(both, None),
            P(both, None),
            P("user", None),
            P("item", None),
            P(both, None),
        ),
        out_specs=(P(both, None), P(both, None), P(both, None), P(both, None)),
        check_vma=False,
    )
```

```python
import functools
import math

import jax
import jax.numpy as jnp
from jax import lax
from jax.experimental import pallas as pl
from jax.experimental.pallas import tpu as pltpu
from jax.sharding import PartitionSpec as P

MESH = pl.DeviceIdType.MESH
F32 = jnp.float32
BF16 = jnp.bfloat16
VMEM_LIMIT = 60 * 1024 * 1024


def up16(rows):
    return (rows + 15) // 16 * 16


def dot(left, right, left_dim, right_dim):
    return lax.dot_general(
        left, right, (((left_dim,), (right_dim,)), ((), ())), preferred_element_type=F32
    )


class Grid:
    def __init__(self, users, items):
        nc = 2 if users % 2 == 0 else 1
        rest = users // nc
        ny = 1
        while rest % (2 * ny) == 0 and (2 * ny) * (2 * ny) <= rest:
            ny *= 2
        self.n = {"z": rest // ny, "y": ny, "c": nc, "x": items}

    def here(self):
        user = lax.axis_index("user")
        n = self.n
        return {
            "c": lax.rem(user, n["c"]),
            "y": lax.rem(lax.div(user, n["c"]), n["y"]),
            "z": lax.div(user, n["c"] * n["y"]),
            "x": lax.axis_index("item"),
        }

    def moved(self, at, **steps):
        out = dict(at)
        for axis, step in steps.items():
            if step:
                out[axis] = lax.rem(at[axis] + step + self.n[axis], self.n[axis])
        return out

    def device(self, at):
        n = self.n
        return ((at["z"] * n["y"] + at["y"]) * n["c"] + at["c"], at["x"])

    def shard(self, at):
        user, item = self.device(at)
        return user * self.n["x"] + item

    def partners(self, at):
        return [
            self.moved(at, **{axis: step})
            for axis in "zycx"
            for step in range(1, self.n[axis])
        ]


def enter(grid, at):
    barrier = pltpu.get_barrier_semaphore()
    others = grid.partners(at)
    for other in others:
        pl.semaphore_signal(barrier, inc=1, device_id=grid.device(other), device_id_type=MESH)
    pl.semaphore_wait(barrier, len(others))


class Wires:
    def __init__(self, grid, send_sems, recv_sems):
        self.grid, self.send, self.recv, self.used, self.copies = grid, send_sems, recv_sems, 0, []

    def start(self, src, dst, to):
        copy = pltpu.make_async_remote_copy(
            src_ref=src,
            dst_ref=dst,
            send_sem=self.send.at[self.used],
            recv_sem=self.recv.at[self.used],
            device_id=self.grid.device(to),
            device_id_type=MESH,
        )
        copy.start()
        self.used += 1
        self.copies.append(copy)
        return copy

    def finish(self):
        for copy in self.copies:
            copy.wait_send()


def halves(rows):
    first = up16(rows // 2)
    return (0, first), (first, rows - first)


def order(n):
    return [(step + 1) % n for step in range(n)]


class GatherFlow:
    def __init__(self, wires, grid, at, ref, part, one, two):
        self.wires, self.grid, self.at, self.ref = wires, grid, at, ref
        self.part, self.one, self.two = part, one, two
        self.z, self.first, self.second, self.core = {}, {}, {}, {}

    def send(self, owner, **to):
        ref = self.ref.at[self.grid.shard(owner), pl.ds(*self.part)]
        return self.wires.start(ref, ref, self.grid.moved(self.at, **to))

    def start(self):
        for dz in range(1, self.grid.n["z"]):
            self.z[dz] = self.send(self.at, z=dz)

    def stage_one(self, dz):
        if dz:
            self.z[dz].wait_recv()
        owner = self.grid.moved(self.at, z=-dz)
        for d1 in range(1, self.grid.n[self.one]):
            self.first[dz, d1] = self.send(owner, **{self.one: d1})

    def stage_two(self, dz):
        for d1 in range(self.grid.n[self.one]):
            if d1:
                self.first[dz, d1].wait_recv()
            owner = self.grid.moved(self.at, **{"z": -dz, self.one: -d1})
            for d2 in range(1, self.grid.n[self.two]):
                self.second[dz, d1, d2] = self.send(owner, **{self.two: d2})

    def stage_core(self, dz):
        for d1 in range(self.grid.n[self.one]):
            for d2 in range(self.grid.n[self.two]):
                if d2:
                    self.second[dz, d1, d2].wait_recv()
                owner = self.grid.moved(self.at, **{"z": -dz, self.one: -d1, self.two: -d2})
                for dc in range(1, self.grid.n["c"]):
                    self.core[dz, d1, d2, dc] = self.send(owner, c=dc)

    def end(self, dz, dc):
        for key, copy in self.core.items():
            if key[0] == dz and key[3] == dc:
                copy.wait_recv()


class ScatterFlow:
    def __init__(self, wires, grid, at, terms, part, one, two, planes):
        self.wires, self.grid, self.at, self.terms = wires, grid, at, terms
        self.part, self.one, self.two, self.planes = part, one, two, planes
        self.core, self.first, self.second, self.z = {}, {}, {}, {}

    def rows(self):
        return pl.ds(*self.part)

    def slot(self, dz, d1, d2):
        n = self.grid.n
        return (dz * n[self.one] + d1) * n[self.two] + d2

    def send(self, name, target, slot, value, **to):
        rows = self.rows()
        self.planes["send_" + name][slot, rows, :] = value.astype(BF16)
        return self.wires.start(
            self.planes["send_" + name].at[slot, rows],
            self.planes["in_" + name].at[slot, rows],
            self.grid.moved(self.at, **to),
        )

    def got(self, name, slot):
        return self.planes["in_" + name][slot, self.rows(), :].astype(F32)

    def each(self):
        n = self.grid.n
        return [(d1, d2) for d1 in range(n[self.one]) for d2 in range(n[self.two])]

    def start(self, dz):
        chip = self.grid.n["z"] * len(self.each())
        for d1, d2 in self.each():
            for dc in range(1, self.grid.n["c"]):
                steps = {"z": dz, self.one: d1, self.two: d2, "c": dc}
                self.core[dz, d1, d2, dc] = self.wires.start(
                    self.terms.at[self.grid.shard(self.grid.moved(self.at, **steps)), self.rows()],
                    self.planes["in_c"].at[(dc - 1) * chip + self.slot(dz, d1, d2), self.rows()],
                    self.grid.moved(self.at, c=dc),
                )

    def stage_one(self, dz):
        chip = self.grid.n["z"] * len(self.each())
        for d1, d2 in reversed(self.each()):
            slot = self.slot(dz, d1, d2)
            own = self.grid.shard(self.grid.moved(self.at, **{"z": dz, self.one: d1, self.two: d2}))
            value = self.terms[own, self.rows(), :].astype(F32)
            for dc in range(1, self.grid.n["c"]):
                self.core[dz, d1, d2, dc].wait_recv()
                value = value + self.got("c", (dc - 1) * chip + slot)
            if d1:
                self.first[dz, d1, d2] = self.send("one", d1, slot, value, **{self.one: d1})
            else:
                self.planes["keep"][dz * self.grid.n[self.two] + d2, self.rows(), :] = value

    def stage_two(self, dz):
        for d2 in reversed(range(self.grid.n[self.two])):
            slot = dz * self.grid.n[self.two] + d2
            value = self.planes["keep"][slot, self.rows(), :]
            for d1 in range(1, self.grid.n[self.one]):
                self.first[dz, d1, d2].wait_recv()
                value = value + self.got("one", self.slot(dz, d1, d2))
            if d2:
                self.second[dz, d2] = self.send("two", d2, slot, value, **{self.two: d2})
            else:
                self.planes["mid"][dz, self.rows(), :] = value

    def stage_three(self, dz):
        value = self.planes["mid"][dz, self.rows(), :]
        for d2 in range(1, self.grid.n[self.two]):
            self.second[dz, d2].wait_recv()
            value = value + self.got("two", dz * self.grid.n[self.two] + d2)
        if dz:
            self.z[dz] = self.send("z", dz, dz, value, z=dz)
        else:
            self.planes["mid"][dz, self.rows(), :] = value

    def end(self):
        value = self.planes["mid"][0, self.rows(), :]
        for dz in range(1, self.grid.n["z"]):
            self.z[dz].wait_recv()
            value = value + self.got("z", dz)
        return value


PLANES = ("in_c", "keep", "send_one", "in_one", "mid", "send_two", "in_two", "send_z", "in_z")


def planes_for(grid, rows, rank):
    n = grid.n
    chip, most = n["z"] * n["y"] * n["x"], n["z"] * max(n["x"], n["y"])
    counts = {
        "in_c": chip * max(n["c"] - 1, 1),
        "send_one": chip,
        "in_one": chip,
        "keep": most,
        "send_two": most,
        "in_two": most,
        "mid": n["z"],
        "send_z": n["z"],
        "in_z": n["z"],
    }
    kind = lambda name: F32 if name in ("keep", "mid") else BF16
    return [pltpu.VMEM((counts[name], rows, rank), kind(name)) for name in PLANES]


def whole_kernel(
    grid, scale,
    user_block_ref, item_block_ref, stratum_ref, ids_ref, observed_hbm, core_ref, user_ref, item_ref,
    context_ref,
    core_out, item_out, ctx_out, user_out,
    observed_ref, wide_ref, item32_ref, cores_ref, first_ref, cube_ref, few_ref, few_terms_ref,
    user_terms_ref, user_in, *rest,
):
    count = len(PLANES)
    big = dict(zip(PLANES, rest[:count]))
    little = dict(zip(PLANES, rest[count:2 * count]))
    load_sem, send_sems, recv_sems = rest[2 * count:]
    n = grid.n
    at = grid.here()
    total, m, rank = cores_ref.shape
    bu, bi, kc = observed_ref.shape
    users = total // n["x"]
    ni, nk = item_ref.shape[0] // users, context_ref.shape[0]
    ni_pad, nk_pad = up16(ni), up16(nk)
    rank_two = rank
    rank_one = total * m // rank_two
    pitch = bi + 8
    group = n["x"] * m
    across = group // rank_two

    load = pltpu.make_async_copy(observed_hbm, observed_ref, load_sem)
    load.start()
    own = grid.shard(at)
    cores_ref[own] = core_ref[...].astype(BF16)
    item32_ref[...] = item_ref[...].astype(F32)
    start = pl.multiple_of(grid.device(at)[0] * ni, ni)

    def padded(value, rows):
        if value.shape[0] == rows:
            return value.astype(BF16)
        fill = jnp.zeros((rows - value.shape[0], rank), F32)
        return jnp.concatenate([value, fill], axis=0).astype(BF16)

    few_ref[own, pl.ds(0, ni_pad), :] = padded(item32_ref[pl.ds(start, ni), :], ni_pad)
    few_ref[own, pl.ds(ni_pad, nk_pad), :] = padded(context_ref[...].astype(F32), nk_pad)
    enter(grid, at)
    wires = Wires(grid, send_sems, recv_sems)
    low, high = halves(m)
    few_part = (0, ni_pad + nk_pad)
    few = GatherFlow(wires, grid, at, few_ref, few_part, "y", "x")
    flows = [
        GatherFlow(wires, grid, at, cores_ref, low, "y", "x"),
        GatherFlow(wires, grid, at, cores_ref, high, "x", "y"),
    ]
    last = n["z"] - 1

    def each(stage, dz):
        if dz <= last:
            for flow in flows:
                getattr(flow, stage)(dz)

    few.start()
    few.stage_one(0)
    for flow in flows:
        flow.start()
    each("stage_one", 0)
    for dz in range(1, n["z"]):
        few.stage_one(dz)
    each("stage_one", 1)
    for dz in range(n["z"]):
        few.stage_two(dz)
    each("stage_two", 0)
    each("stage_one", 2)
    for dz in range(n["z"]):
        few.stage_core(dz)
    each("stage_two", 1)
    load.wait()

    def widen(a, carry):
        row = pl.multiple_of(a * pitch, 8)
        wide_ref[pl.ds(row, bi), :] = observed_ref[a].astype(F32)
        return carry

    lax.fori_loop(0, bu, widen, 0, unroll=4)
    each("stage_one", 3)
    each("stage_two", 2)
    for dz in range(n["z"]):
        for dc in range(1, n["c"]):
            few.end(dz, dc)

    user_block, item_block, stratum = user_block_ref[0], item_block_ref[0], stratum_ref[0]
    blocks = item_ref.shape[0] // bi
    chosen = jnp.full((bu, rank), user_block, jnp.int32)
    user32 = jnp.zeros((bu, rank), F32)
    for j in range(user_ref.shape[0] // bu):
        user32 = jnp.where(chosen == j, user_ref[pl.ds(j * bu, bu), :].astype(F32), user32)
    user_rows, user_turned = user32.astype(BF16), user32.T.astype(BF16)
    chosen = jnp.full((bi, rank), stratum * blocks + item_block, jnp.int32)
    item32 = jnp.zeros((bi, rank), F32)
    for block in range(n["x"] * blocks):
        begin = (block % blocks) * (bi // ni) * n["x"] + block // blocks
        rows = jnp.concatenate(
            [
                few_ref[begin + j * n["x"], pl.ds(0, ni_pad), :].astype(F32)[:ni]
                for j in range(bi // ni)
            ],
            axis=0,
        )
        item32 = jnp.where(chosen == block, rows, item32)
    item_rows, item_turned = item32.astype(BF16), item32.T.astype(BF16)
    ids = ids_ref[...]
    places = lax.div(ids, jnp.full_like(ids, nk)) * nk_pad + lax.rem(ids, jnp.full_like(ids, nk))
    spots = lax.broadcasted_iota(jnp.int32, (total * nk_pad, kc), 0)
    picker = jnp.where(spots == places, 1.0, 0.0).astype(BF16)
    ctx_all = few_ref[:, pl.ds(ni_pad, nk_pad), :].reshape(total * nk_pad, rank)
    ctx32 = dot(picker, ctx_all, 0, 0)
    ctx_rows, ctx_turned = ctx32.astype(BF16), ctx32.T.astype(BF16)

    def first_shard(dz, dy, dc):
        z = lax.rem(at["z"] + dz + n["z"], n["z"])
        y = lax.rem(at["y"] + dy, n["y"])
        c = lax.rem(at["c"] + dc, n["c"])
        return ((z * n["y"] + y) * n["c"] + c) * n["x"]

    def forward(dz, dc):
        def step(dy, carry):
            shard = first_shard(-dz, dy, dc)
            core = cores_ref[pl.ds(shard, n["x"]), :, :].reshape(group, rank)
            first = dot(core, ctx_turned, 1, 0).astype(BF16)
            row = pl.multiple_of(shard * m, group)
            first_ref[pl.ds(row, group), :] = first
            wide = jnp.concatenate(
                [first[j * rank_two:(j + 1) * rank_two] for j in range(across)], axis=1
            )
            second = dot(item_rows, wide, 1, 0)
            p = lax.div(shard * m, rank_two)
            for j in range(across):
                cube_ref[pl.ds(pl.multiple_of((p + j) * pitch, 8), bi), :] = (
                    second[:, j * kc:(j + 1) * kc]
                )
            return carry

        lax.fori_loop(0, n["y"], step, 0)

    for k in range(n["z"] + 1):
        each("stage_core", k)
        if k <= last:
            forward(k, 0)
        if k + 4 <= last:
            each("stage_one", k + 4)
        if k + 3 <= last:
            each("stage_two", k + 3)
        if k >= 1:
            for dc in range(1, n["c"]):
                for flow in flows:
                    flow.end(k - 1, dc)
                forward(k - 1, dc)

    wide_b = 8

    def middle(k, grad_user):
        b = k * wide_b
        second = jnp.concatenate(
            [cube_ref[pl.ds(b + j, rank_one, stride=pitch), :].astype(BF16) for j in range(wide_b)],
            axis=1,
        )
        seen = jnp.concatenate(
            [wide_ref[pl.ds(b + j, bu, stride=pitch), :] for j in range(wide_b)], axis=1
        )
        residual = (dot(user_rows, second, 1, 0) - seen).astype(BF16)
        back = dot(user_turned, residual, 1, 0)
        for j in range(wide_b):
            cube_ref[pl.ds(b + j, rank_one, stride=pitch), :] = back[:, j * kc:(j + 1) * kc]
        return grad_user + dot(residual, second, 1, 1)

    grad_user = lax.fori_loop(0, bi // wide_b, middle, jnp.zeros((bu, rank_one), F32))
    grad_user = grad_user * scale
    for j in range(user_ref.shape[0] // bu):
        here = jnp.full(grad_user.shape, user_block, jnp.int32) == j
        user_terms_ref[pl.ds(j * bu, bu), :] = jnp.where(here, grad_user, 0.0)
    wires.finish()
    wires.copies = []

    chunk = user_out.shape[0]
    user_copies = []
    for dx in range(1, n["x"]):
        to = grid.moved(at, x=dx)
        start = pl.multiple_of(to["x"] * chunk, chunk)
        user_copies.append(
            wires.start(user_terms_ref.at[pl.ds(start, chunk)], user_in.at[dx - 1], to)
        )

    sums = [
        ScatterFlow(wires, grid, at, cores_ref, low, "x", "y", big),
        ScatterFlow(wires, grid, at, cores_ref, high, "y", "x", big),
    ]

    def backward(dz, dc, carry):
        def step(dy, carry):
            grad_item, grad_ctx = carry
            shard = first_shard(dz, dy, dc)
            p = lax.div(shard * m, rank_two)
            row = pl.multiple_of(shard * m, group)
            core = cores_ref[pl.ds(shard, n["x"]), :, :].reshape(group, rank)
            wide = jnp.concatenate(
                [
                    cube_ref[pl.ds(pl.multiple_of((p + j) * pitch, 8), bi), :].astype(BF16)
                    for j in range(across)
                ],
                axis=1,
            )
            first = first_ref[pl.ds(row, group), :]
            first = jnp.concatenate(
                [first[j * rank_two:(j + 1) * rank_two] for j in range(across)], axis=1
            )
            grad_item = grad_item + dot(wide, first, 1, 1)
            folded = dot(item_turned, wide, 1, 0).astype(BF16)
            folded = jnp.concatenate(
                [folded[:, j * kc:(j + 1) * kc] for j in range(across)], axis=0
            )
            grad_ctx = grad_ctx + dot(folded, core, 0, 0)
            grad_core = (dot(folded, ctx_rows, 1, 0) * scale).astype(BF16)
            cores_ref[pl.ds(shard, n["x"]), :, :] = grad_core.reshape(n["x"], m, rank)
            return grad_item, grad_ctx

        return lax.fori_loop(0, n["y"], step, carry)

    carry = (jnp.zeros((bi, rank_two), F32), jnp.zeros((kc, rank), F32))
    turns = order(n["z"])
    for k, dz in enumerate(turns):
        for dc in range(1, n["c"]):
            carry = backward(dz, dc, carry)
        for flow in sums:
            flow.start(dz)
        carry = backward(dz, 0, carry)
        for flow in sums:
            flow.stage_one(dz)
        if k >= 1:
            for flow in sums:
                flow.stage_two(turns[k - 1])
        if k >= 2:
            for flow in sums:
                flow.stage_three(turns[k - 2])

    grad_item, grad_ctx = carry
    grad_item, grad_ctx = grad_item * scale, grad_ctx * scale
    mine = jnp.full((ni_pad, rank), stratum * blocks + item_block, jnp.int32)
    for block in range(n["x"] * blocks):
        for j in range(bi // ni):
            piece = padded(grad_item[j * ni:(j + 1) * ni], ni_pad).astype(F32)
            few_terms_ref[block * (bi // ni) + j, pl.ds(0, ni_pad), :] = (
                jnp.where(mine == block, piece, 0.0).astype(BF16)
            )
    upper = grad_ctx.astype(BF16)
    lower = (grad_ctx - upper.astype(F32)).astype(BF16)
    spread = dot(picker, upper, 1, 0) + dot(picker, lower, 1, 0)
    few_terms_ref[:, pl.ds(ni_pad, nk_pad), :] = spread.astype(BF16).reshape(total, nk_pad, rank)
    few_sums = ScatterFlow(wires, grid, at, few_terms_ref, few_part, "x", "y", little)
    for dz in turns:
        few_sums.start(dz)
    if len(turns) >= 2:
        for flow in sums:
            flow.stage_three(turns[-2])
    for dz in turns:
        few_sums.stage_one(dz)
    for flow in sums:
        flow.stage_two(turns[-1])
    for dz in turns:
        few_sums.stage_two(dz)
    for flow in sums:
        flow.stage_three(turns[-1])
    for dz in turns:
        few_sums.stage_three(dz)

    value = user_terms_ref[pl.ds(pl.multiple_of(at["x"] * chunk, chunk), chunk), :]
    for dx, copy in enumerate(user_copies):
        copy.wait_recv()
        value = value + user_in[dx]
    user_out[...] = value
    for flow in sums:
        core_out[pl.ds(*flow.part), :] = flow.end()
    value = few_sums.end()
    item_out[...] = value[:ni]
    ctx_out[...] = value[ni_pad:ni_pad + nk]
    wires.finish()


def whole(grid, scale, user_block, item_block, stratum, ids, observed, core, users, items, contexts):
    n = grid.n
    total = n["z"] * n["y"] * n["c"] * n["x"]
    bu, bi, kc = observed.shape
    m, rank = core.shape
    ni, nk = items.shape[0] // (total // n["x"]), contexts.shape[0]
    few = up16(ni) + up16(nk)
    chunk = users.shape[0] // n["x"]
    copies = 6 * total + n["x"]
    pitch = bi + 8
    vmem, smem = pl.BlockSpec(memory_space=pltpu.VMEM), pl.BlockSpec(memory_space=pltpu.SMEM)
    return pl.pallas_call(
        functools.partial(whole_kernel, grid, scale),
        out_shape=tuple(
            jax.ShapeDtypeStruct((count, rank), F32) for count in (m, ni, nk, chunk)
        ),
        in_specs=[smem] * 3 + [vmem, pl.BlockSpec(memory_space=pl.ANY)] + [vmem] * 4,
        out_specs=(vmem,) * 4,
        scratch_shapes=[
            pltpu.VMEM((bu, bi, kc), BF16),
            pltpu.VMEM((bu * pitch, kc), F32),
            pltpu.VMEM(items.shape, F32),
            pltpu.VMEM((total, m, rank), BF16),
            pltpu.VMEM((total * m, kc), BF16),
            pltpu.VMEM((total * m // rank * pitch, kc), F32),
            pltpu.VMEM((total, few, rank), BF16),
            pltpu.VMEM((total, few, rank), BF16),
            pltpu.VMEM(users.shape, F32),
            pltpu.VMEM((max(n["x"] - 1, 1), chunk, rank), F32),
            *planes_for(grid, m, rank),
            *planes_for(grid, few, rank),
            pltpu.SemaphoreType.DMA,
            pltpu.SemaphoreType.DMA((copies,)),
            pltpu.SemaphoreType.DMA((copies,)),
        ],
        compiler_params=pltpu.CompilerParams(
            collective_id=0, has_side_effects=True, vmem_limit_bytes=VMEM_LIMIT
        ),
        cost_estimate=pl.CostEstimate(
            flops=9 * 2 * total * m * bi * kc, bytes_accessed=observed.size * 2, transcendentals=0
        ),
        name="tucker_gradient",
    )(user_block, item_block, stratum, ids, observed, core, users, items, contexts)


def hand_over_kernel(*refs):
    half = len(refs) // 2
    for source, target in zip(refs[:half], refs[half:]):
        target[...] = source[...]


def hand_over(arrays):
    vmem = pl.BlockSpec(memory_space=pltpu.VMEM)
    return pl.pallas_call(
        hand_over_kernel,
        out_shape=tuple(jax.ShapeDtypeStruct(a.shape, a.dtype) for a in arrays),
        in_specs=[vmem] * len(arrays),
        out_specs=(vmem,) * len(arrays),
        name="hand_over",
    )(*arrays)


def local(
    grid, observed, user_block, item_block, stratum, context_ids, core_tensor, user_factor,
    item_factor, context_factor,
):
    tiles_here, block_user, block_item, slices = observed.shape
    scale = 1.0 / math.sqrt(block_user * block_item * slices)
    sums = None
    for t in range(tiles_here):
        one = slice(t, t + 1)
        terms = whole(
            grid, scale, user_block[one], item_block[one], stratum[one], context_ids[one],
            observed[t], core_tensor, user_factor, item_factor, context_factor,
        )
        sums = terms if sums is None else tuple(a + b for a, b in zip(sums, terms))
    core_grad, item_grad, context_grad, user_grad = hand_over(sums)
    return (core_grad, user_grad, item_grad, context_grad)


def solution(mesh):
    grid = Grid(mesh.shape["user"], mesh.shape["item"])
    both = ("user", "item")
    return jax.shard_map(
        functools.partial(local, grid),
        mesh=mesh,
        in_specs=(
            P(both, None, None, None),
            P(both),
            P(both),
            P(both),
            P(both, None),
            P(both, None),
            P("user", None),
            P("item", None),
            P(both, None),
        ),
        out_specs=(P(both, None), P(both, None), P(both, None), P(both, None)),
        check_vma=False,
    )
```

```python
import functools
import math

import jax
import jax.numpy as jnp
from jax import lax
from jax.experimental import pallas as pl
from jax.experimental.pallas import tpu as pltpu
from jax.sharding import PartitionSpec as P

MESH = pl.DeviceIdType.MESH
F32 = jnp.float32
BF16 = jnp.bfloat16
VMEM_LIMIT = 60 * 1024 * 1024


def up16(rows):
    return (rows + 15) // 16 * 16


def dot(left, right, left_dim, right_dim):
    return lax.dot_general(
        left, right, (((left_dim,), (right_dim,)), ((), ())), preferred_element_type=F32
    )


class Grid:
    def __init__(self, users, items):
        nc = 2 if users % 2 == 0 else 1
        rest = users // nc
        ny = 1
        while rest % (2 * ny) == 0 and (2 * ny) * (2 * ny) <= rest:
            ny *= 2
        self.n = {"z": rest // ny, "y": ny, "c": nc, "x": items}

    def here(self):
        user = lax.axis_index("user")
        n = self.n
        return {
            "c": lax.rem(user, n["c"]),
            "y": lax.rem(lax.div(user, n["c"]), n["y"]),
            "z": lax.div(user, n["c"] * n["y"]),
            "x": lax.axis_index("item"),
        }

    def moved(self, at, **steps):
        out = dict(at)
        for axis, step in steps.items():
            if step:
                out[axis] = lax.rem(at[axis] + step + self.n[axis], self.n[axis])
        return out

    def device(self, at):
        n = self.n
        return ((at["z"] * n["y"] + at["y"]) * n["c"] + at["c"], at["x"])

    def shard(self, at):
        user, item = self.device(at)
        return user * self.n["x"] + item

    def partners(self, at):
        return [
            self.moved(at, **{axis: step})
            for axis in "zycx"
            for step in range(1, self.n[axis])
        ]


def enter(grid, at):
    barrier = pltpu.get_barrier_semaphore()
    others = grid.partners(at)
    for other in others:
        pl.semaphore_signal(barrier, inc=1, device_id=grid.device(other), device_id_type=MESH)
    pl.semaphore_wait(barrier, len(others))


class Wires:
    def __init__(self, grid, send_sems, recv_sems):
        self.grid, self.send, self.recv, self.used, self.copies = grid, send_sems, recv_sems, 0, []

    def start(self, src, dst, to):
        copy = pltpu.make_async_remote_copy(
            src_ref=src,
            dst_ref=dst,
            send_sem=self.send.at[self.used],
            recv_sem=self.recv.at[self.used],
            device_id=self.grid.device(to),
            device_id_type=MESH,
        )
        copy.start()
        self.used += 1
        self.copies.append(copy)
        return copy

    def finish(self):
        for copy in self.copies:
            copy.wait_send()


def halves(rows):
    first = up16(rows // 2)
    return (0, first), (first, rows - first)


def order(n):
    return [(step + 1) % n for step in range(n)]


class GatherFlow:
    def __init__(self, wires, grid, at, ref, part, one, two):
        self.wires, self.grid, self.at, self.ref = wires, grid, at, ref
        self.part, self.one, self.two = part, one, two
        self.z, self.first, self.second, self.core = {}, {}, {}, {}

    def send(self, owner, **to):
        ref = self.ref.at[self.grid.shard(owner), pl.ds(*self.part)]
        return self.wires.start(ref, ref, self.grid.moved(self.at, **to))

    def start(self):
        for dz in range(1, self.grid.n["z"]):
            self.z[dz] = self.send(self.at, z=dz)

    def stage_one(self, dz):
        if dz:
            self.z[dz].wait_recv()
        owner = self.grid.moved(self.at, z=-dz)
        for d1 in range(1, self.grid.n[self.one]):
            self.first[dz, d1] = self.send(owner, **{self.one: d1})

    def stage_two(self, dz):
        for d1 in range(self.grid.n[self.one]):
            if d1:
                self.first[dz, d1].wait_recv()
            owner = self.grid.moved(self.at, **{"z": -dz, self.one: -d1})
            for d2 in range(1, self.grid.n[self.two]):
                self.second[dz, d1, d2] = self.send(owner, **{self.two: d2})

    def stage_core(self, dz):
        for d1 in range(self.grid.n[self.one]):
            for d2 in range(self.grid.n[self.two]):
                if d2:
                    self.second[dz, d1, d2].wait_recv()
                owner = self.grid.moved(self.at, **{"z": -dz, self.one: -d1, self.two: -d2})
                for dc in range(1, self.grid.n["c"]):
                    self.core[dz, d1, d2, dc] = self.send(owner, c=dc)

    def end(self, dz, dc):
        for key, copy in self.core.items():
            if key[0] == dz and key[3] == dc:
                copy.wait_recv()


class ScatterFlow:
    def __init__(self, wires, grid, at, terms, part, one, two, planes):
        self.wires, self.grid, self.at, self.terms = wires, grid, at, terms
        self.part, self.one, self.two, self.planes = part, one, two, planes
        self.core, self.first, self.second, self.z = {}, {}, {}, {}

    def rows(self):
        return pl.ds(*self.part)

    def slot(self, dz, d1, d2):
        n = self.grid.n
        return (dz * n[self.one] + d1) * n[self.two] + d2

    def send(self, name, target, slot, value, **to):
        rows = self.rows()
        self.planes["send_" + name][slot, rows, :] = value.astype(BF16)
        return self.wires.start(
            self.planes["send_" + name].at[slot, rows],
            self.planes["in_" + name].at[slot, rows],
            self.grid.moved(self.at, **to),
        )

    def got(self, name, slot):
        return self.planes["in_" + name][slot, self.rows(), :].astype(F32)

    def each(self):
        n = self.grid.n
        return [(d1, d2) for d1 in range(n[self.one]) for d2 in range(n[self.two])]

    def start(self, dz):
        chip = self.grid.n["z"] * len(self.each())
        for d1, d2 in self.each():
            for dc in range(1, self.grid.n["c"]):
                steps = {"z": dz, self.one: d1, self.two: d2, "c": dc}
                self.core[dz, d1, d2, dc] = self.wires.start(
                    self.terms.at[self.grid.shard(self.grid.moved(self.at, **steps)), self.rows()],
                    self.planes["in_c"].at[(dc - 1) * chip + self.slot(dz, d1, d2), self.rows()],
                    self.grid.moved(self.at, c=dc),
                )

    def stage_one(self, dz):
        chip = self.grid.n["z"] * len(self.each())
        for d1, d2 in reversed(self.each()):
            slot = self.slot(dz, d1, d2)
            own = self.grid.shard(self.grid.moved(self.at, **{"z": dz, self.one: d1, self.two: d2}))
            value = self.terms[own, self.rows(), :].astype(F32)
            for dc in range(1, self.grid.n["c"]):
                self.core[dz, d1, d2, dc].wait_recv()
                value = value + self.got("c", (dc - 1) * chip + slot)
            if d1:
                self.first[dz, d1, d2] = self.send("one", d1, slot, value, **{self.one: d1})
            else:
                self.planes["keep"][dz * self.grid.n[self.two] + d2, self.rows(), :] = value

    def stage_two(self, dz):
        for d2 in reversed(range(self.grid.n[self.two])):
            slot = dz * self.grid.n[self.two] + d2
            value = self.planes["keep"][slot, self.rows(), :]
            for d1 in range(1, self.grid.n[self.one]):
                self.first[dz, d1, d2].wait_recv()
                value = value + self.got("one", self.slot(dz, d1, d2))
            if d2:
                self.second[dz, d2] = self.send("two", d2, slot, value, **{self.two: d2})
            else:
                self.planes["mid"][dz, self.rows(), :] = value

    def stage_three(self, dz):
        value = self.planes["mid"][dz, self.rows(), :]
        for d2 in range(1, self.grid.n[self.two]):
            self.second[dz, d2].wait_recv()
            value = value + self.got("two", dz * self.grid.n[self.two] + d2)
        if dz:
            self.z[dz] = self.send("z", dz, dz, value, z=dz)
        else:
            self.planes["mid"][dz, self.rows(), :] = value

    def end(self):
        value = self.planes["mid"][0, self.rows(), :]
        for dz in range(1, self.grid.n["z"]):
            self.z[dz].wait_recv()
            value = value + self.got("z", dz)
        return value


PLANES = ("in_c", "keep", "send_one", "in_one", "mid", "send_two", "in_two", "send_z", "in_z")


def planes_for(grid, rows, rank):
    n = grid.n
    chip, most = n["z"] * n["y"] * n["x"], n["z"] * max(n["x"], n["y"])
    counts = {
        "in_c": chip * max(n["c"] - 1, 1),
        "send_one": chip,
        "in_one": chip,
        "keep": most,
        "send_two": most,
        "in_two": most,
        "mid": n["z"],
        "send_z": n["z"],
        "in_z": n["z"],
    }
    kind = lambda name: F32 if name in ("keep", "mid") else BF16
    return [pltpu.VMEM((counts[name], rows, rank), kind(name)) for name in PLANES]


def whole_kernel(
    grid, scale,
    user_block_ref, item_block_ref, stratum_ref, ids_ref, observed_hbm, core_ref, user_ref, item_ref,
    context_ref,
    core_out, item_out, ctx_out, user_out,
    observed_ref, wide_ref, item32_ref, cores_ref, first_ref, cube_ref, few_ref, few_terms_ref,
    user_terms_ref, user_in, *rest,
):
    count = len(PLANES)
    big = dict(zip(PLANES, rest[:count]))
    little = dict(zip(PLANES, rest[count:2 * count]))
    load_sem, send_sems, recv_sems = rest[2 * count:]
    n = grid.n
    at = grid.here()
    total, m, rank = cores_ref.shape
    bu, bi, kc = observed_ref.shape
    users = total // n["x"]
    ni, nk = item_ref.shape[0] // users, context_ref.shape[0]
    ni_pad, nk_pad = up16(ni), up16(nk)
    rank_two = rank
    rank_one = total * m // rank_two
    pitch = bi + 8
    group = n["x"] * m
    across = group // rank_two

    load = pltpu.make_async_copy(observed_hbm, observed_ref, load_sem)
    load.start()
    own = grid.shard(at)
    cores_ref[own] = core_ref[...].astype(BF16)
    item32_ref[...] = item_ref[...].astype(F32)
    start = pl.multiple_of(grid.device(at)[0] * ni, ni)

    def padded(value, rows):
        if value.shape[0] == rows:
            return value.astype(BF16)
        fill = jnp.zeros((rows - value.shape[0], rank), F32)
        return jnp.concatenate([value, fill], axis=0).astype(BF16)

    few_ref[own, pl.ds(0, ni_pad), :] = padded(item32_ref[pl.ds(start, ni), :], ni_pad)
    few_ref[own, pl.ds(ni_pad, nk_pad), :] = padded(context_ref[...].astype(F32), nk_pad)
    enter(grid, at)
    wires = Wires(grid, send_sems, recv_sems)
    low, high = halves(m)
    few_part = (0, ni_pad + nk_pad)
    few = GatherFlow(wires, grid, at, few_ref, few_part, "y", "x")
    flows = [
        GatherFlow(wires, grid, at, cores_ref, low, "y", "x"),
        GatherFlow(wires, grid, at, cores_ref, high, "x", "y"),
    ]
    few.start()
    few.stage_one(0)
    for flow in flows:
        flow.start()
    for flow in flows:
        flow.stage_one(0)
    for dz in range(1, n["z"]):
        few.stage_one(dz)
    load.wait()

    def widen(a, carry):
        row = pl.multiple_of(a * pitch, 8)
        wide_ref[pl.ds(row, bi), :] = observed_ref[a].astype(F32)
        return carry

    lax.fori_loop(0, bu, widen, 0, unroll=4)
    for dz in range(n["z"]):
        few.stage_two(dz)
    for flow in flows:
        flow.stage_two(0)
    for dz in range(n["z"]):
        few.stage_core(dz)
    if n["z"] > 1:
        for flow in flows:
            flow.stage_one(1)
    for dz in range(n["z"]):
        for dc in range(1, n["c"]):
            few.end(dz, dc)

    user_block, item_block, stratum = user_block_ref[0], item_block_ref[0], stratum_ref[0]
    blocks = item_ref.shape[0] // bi
    chosen = jnp.full((bu, rank), user_block, jnp.int32)
    user32 = jnp.zeros((bu, rank), F32)
    for j in range(user_ref.shape[0] // bu):
        user32 = jnp.where(chosen == j, user_ref[pl.ds(j * bu, bu), :].astype(F32), user32)
    user_rows, user_turned = user32.astype(BF16), user32.T.astype(BF16)
    chosen = jnp.full((bi, rank), stratum * blocks + item_block, jnp.int32)
    item32 = jnp.zeros((bi, rank), F32)
    for block in range(n["x"] * blocks):
        begin = (block % blocks) * (bi // ni) * n["x"] + block // blocks
        rows = jnp.concatenate(
            [
                few_ref[begin + j * n["x"], pl.ds(0, ni_pad), :].astype(F32)[:ni]
                for j in range(bi // ni)
            ],
            axis=0,
        )
        item32 = jnp.where(chosen == block, rows, item32)
    item_rows, item_turned = item32.astype(BF16), item32.T.astype(BF16)
    ids = ids_ref[...]
    places = lax.div(ids, jnp.full_like(ids, nk)) * nk_pad + lax.rem(ids, jnp.full_like(ids, nk))
    spots = lax.broadcasted_iota(jnp.int32, (total * nk_pad, kc), 0)
    picker = jnp.where(spots == places, 1.0, 0.0).astype(BF16)
    ctx_all = few_ref[:, pl.ds(ni_pad, nk_pad), :].reshape(total * nk_pad, rank)
    ctx32 = dot(picker, ctx_all, 0, 0)
    ctx_rows, ctx_turned = ctx32.astype(BF16), ctx32.T.astype(BF16)

    def first_shard(dz, dy, dc):
        z = lax.rem(at["z"] + dz + n["z"], n["z"])
        y = lax.rem(at["y"] + dy, n["y"])
        c = lax.rem(at["c"] + dc, n["c"])
        return ((z * n["y"] + y) * n["c"] + c) * n["x"]

    def lanes(value):
        blocks_here = value.shape[0] // rank_two
        return jnp.concatenate(
            [value[j * rank_two:(j + 1) * rank_two] for j in range(blocks_here)], axis=1
        )

    def cores_at(shards):
        return jnp.concatenate(
            [cores_ref[pl.ds(s, n["x"]), :, :].reshape(group, rank) for s in shards], axis=0
        )

    def forward(dz, dc):
        shards = [first_shard(-dz, dy, dc) for dy in range(n["y"])]
        first = dot(cores_at(shards), ctx_turned, 1, 0).astype(BF16)
        second = dot(item_rows, lanes(first), 1, 0)
        for i, shard in enumerate(shards):
            row = pl.multiple_of(shard * m, group)
            first_ref[pl.ds(row, group), :] = first[i * group:(i + 1) * group]
            p = lax.div(shard * m, rank_two)
            for j in range(across):
                column = (i * across + j) * kc
                cube_ref[pl.ds(pl.multiple_of((p + j) * pitch, 8), bi), :] = (
                    second[:, column:column + kc]
                )

    last = n["z"] - 1
    for k in range(n["z"] + 3):
        if 2 <= k <= last:
            for flow in flows:
                flow.stage_one(k)
        if 1 <= k - 1 <= last:
            for flow in flows:
                flow.stage_two(k - 1)
        if 0 <= k - 2 <= last:
            for flow in flows:
                flow.stage_core(k - 2)
            forward(k - 2, 0)
        if 0 <= k - 3 <= last:
            for dc in range(1, n["c"]):
                for flow in flows:
                    flow.end(k - 3, dc)
                forward(k - 3, dc)

    wide_b = 16 if bi % 16 == 0 else 8

    def middle(k, grad_user):
        b = k * wide_b
        second = jnp.concatenate(
            [cube_ref[pl.ds(b + j, rank_one, stride=pitch), :].astype(BF16) for j in range(wide_b)],
            axis=1,
        )
        seen = jnp.concatenate(
            [wide_ref[pl.ds(b + j, bu, stride=pitch), :] for j in range(wide_b)], axis=1
        )
        residual = (dot(user_rows, second, 1, 0) - seen).astype(BF16)
        back = dot(user_turned, residual, 1, 0)
        for j in range(wide_b):
            cube_ref[pl.ds(b + j, rank_one, stride=pitch), :] = back[:, j * kc:(j + 1) * kc]
        return grad_user + dot(residual, second, 1, 1)

    grad_user = lax.fori_loop(0, bi // wide_b, middle, jnp.zeros((bu, rank_one), F32))
    grad_user = grad_user * scale
    for j in range(user_ref.shape[0] // bu):
        here = jnp.full(grad_user.shape, user_block, jnp.int32) == j
        user_terms_ref[pl.ds(j * bu, bu), :] = jnp.where(here, grad_user, 0.0)
    wires.finish()
    wires.copies = []

    chunk = user_out.shape[0]
    user_copies = []
    for dx in range(1, n["x"]):
        to = grid.moved(at, x=dx)
        start = pl.multiple_of(to["x"] * chunk, chunk)
        user_copies.append(
            wires.start(user_terms_ref.at[pl.ds(start, chunk)], user_in.at[dx - 1], to)
        )

    sums = [
        ScatterFlow(wires, grid, at, cores_ref, low, "x", "y", big),
        ScatterFlow(wires, grid, at, cores_ref, high, "y", "x", big),
    ]

    def backward(dz, dc, carry):
        grad_item, grad_ctx = carry
        shards = [first_shard(dz, dy, dc) for dy in range(n["y"])]
        starts = [lax.div(shard * m, rank_two) for shard in shards]
        core = cores_at(shards)
        wide = jnp.concatenate(
            [
                cube_ref[pl.ds(pl.multiple_of((p + j) * pitch, 8), bi), :].astype(BF16)
                for p in starts
                for j in range(across)
            ],
            axis=1,
        )
        first = [first_ref[pl.ds(pl.multiple_of(s * m, group), group), :] for s in shards]
        folded = dot(item_turned, wide, 1, 0).astype(BF16)
        folded = jnp.concatenate(
            [folded[:, j * kc:(j + 1) * kc] for j in range(folded.shape[1] // kc)], axis=0
        )
        grad_core = (dot(folded, ctx_rows, 1, 0) * scale).astype(BF16)
        for i, shard in enumerate(shards):
            cores_ref[pl.ds(shard, n["x"]), :, :] = (
                grad_core[i * group:(i + 1) * group].reshape(n["x"], m, rank)
            )
        grad_item = grad_item + dot(wide, lanes(jnp.concatenate(first, axis=0)), 1, 1)
        grad_ctx = grad_ctx + dot(folded, core, 0, 0)
        return grad_item, grad_ctx

    carry = (jnp.zeros((bi, rank_two), F32), jnp.zeros((kc, rank), F32))
    turns = order(n["z"])
    for k, dz in enumerate(turns):
        for dc in range(1, n["c"]):
            carry = backward(dz, dc, carry)
        for flow in sums:
            flow.start(dz)
        carry = backward(dz, 0, carry)
        for flow in sums:
            flow.stage_one(dz)
        if k >= 1:
            for flow in sums:
                flow.stage_two(turns[k - 1])
        if k >= 2:
            for flow in sums:
                flow.stage_three(turns[k - 2])

    grad_item, grad_ctx = carry
    grad_item, grad_ctx = grad_item * scale, grad_ctx * scale
    mine = jnp.full((ni_pad, rank), stratum * blocks + item_block, jnp.int32)
    for block in range(n["x"] * blocks):
        for j in range(bi // ni):
            piece = padded(grad_item[j * ni:(j + 1) * ni], ni_pad).astype(F32)
            few_terms_ref[block * (bi // ni) + j, pl.ds(0, ni_pad), :] = (
                jnp.where(mine == block, piece, 0.0).astype(BF16)
            )
    upper = grad_ctx.astype(BF16)
    lower = (grad_ctx - upper.astype(F32)).astype(BF16)
    spread = dot(picker, upper, 1, 0) + dot(picker, lower, 1, 0)
    few_terms_ref[:, pl.ds(ni_pad, nk_pad), :] = spread.astype(BF16).reshape(total, nk_pad, rank)
    few_sums = ScatterFlow(wires, grid, at, few_terms_ref, few_part, "x", "y", little)
    for dz in turns:
        few_sums.start(dz)
    if len(turns) >= 2:
        for flow in sums:
            flow.stage_three(turns[-2])
    for dz in turns:
        few_sums.stage_one(dz)
    for flow in sums:
        flow.stage_two(turns[-1])
    for dz in turns:
        few_sums.stage_two(dz)
    for flow in sums:
        flow.stage_three(turns[-1])
    for dz in turns:
        few_sums.stage_three(dz)

    value = user_terms_ref[pl.ds(pl.multiple_of(at["x"] * chunk, chunk), chunk), :]
    for dx, copy in enumerate(user_copies):
        copy.wait_recv()
        value = value + user_in[dx]
    user_out[...] = value
    for flow in sums:
        core_out[pl.ds(*flow.part), :] = flow.end()
    value = few_sums.end()
    item_out[...] = value[:ni]
    ctx_out[...] = value[ni_pad:ni_pad + nk]
    wires.finish()


def whole(grid, scale, user_block, item_block, stratum, ids, observed, core, users, items, contexts):
    n = grid.n
    total = n["z"] * n["y"] * n["c"] * n["x"]
    bu, bi, kc = observed.shape
    m, rank = core.shape
    ni, nk = items.shape[0] // (total // n["x"]), contexts.shape[0]
    few = up16(ni) + up16(nk)
    chunk = users.shape[0] // n["x"]
    copies = 6 * total + n["x"]
    pitch = bi + 8
    vmem, smem = pl.BlockSpec(memory_space=pltpu.VMEM), pl.BlockSpec(memory_space=pltpu.SMEM)
    return pl.pallas_call(
        functools.partial(whole_kernel, grid, scale),
        out_shape=tuple(
            jax.ShapeDtypeStruct((count, rank), F32) for count in (m, ni, nk, chunk)
        ),
        in_specs=[smem] * 3 + [vmem, pl.BlockSpec(memory_space=pl.ANY)] + [vmem] * 4,
        out_specs=(vmem,) * 4,
        scratch_shapes=[
            pltpu.VMEM((bu, bi, kc), BF16),
            pltpu.VMEM((bu * pitch, kc), F32),
            pltpu.VMEM(items.shape, F32),
            pltpu.VMEM((total, m, rank), BF16),
            pltpu.VMEM((total * m, kc), BF16),
            pltpu.VMEM((total * m // rank * pitch, kc), F32),
            pltpu.VMEM((total, few, rank), BF16),
            pltpu.VMEM((total, few, rank), BF16),
            pltpu.VMEM(users.shape, F32),
            pltpu.VMEM((max(n["x"] - 1, 1), chunk, rank), F32),
            *planes_for(grid, m, rank),
            *planes_for(grid, few, rank),
            pltpu.SemaphoreType.DMA,
            pltpu.SemaphoreType.DMA((copies,)),
            pltpu.SemaphoreType.DMA((copies,)),
        ],
        compiler_params=pltpu.CompilerParams(
            collective_id=0, has_side_effects=True, vmem_limit_bytes=VMEM_LIMIT
        ),
        cost_estimate=pl.CostEstimate(
            flops=9 * 2 * total * m * bi * kc, bytes_accessed=observed.size * 2, transcendentals=0
        ),
        name="tucker_gradient",
    )(user_block, item_block, stratum, ids, observed, core, users, items, contexts)


def hand_over_kernel(*refs):
    half = len(refs) // 2
    for source, target in zip(refs[:half], refs[half:]):
        target[...] = source[...]


def hand_over(arrays):
    vmem = pl.BlockSpec(memory_space=pltpu.VMEM)
    return pl.pallas_call(
        hand_over_kernel,
        out_shape=tuple(jax.ShapeDtypeStruct(a.shape, a.dtype) for a in arrays),
        in_specs=[vmem] * len(arrays),
        out_specs=(vmem,) * len(arrays),
        name="hand_over",
    )(*arrays)


def local(
    grid, observed, user_block, item_block, stratum, context_ids, core_tensor, user_factor,
    item_factor, context_factor,
):
    tiles_here, block_user, block_item, slices = observed.shape
    scale = 1.0 / math.sqrt(block_user * block_item * slices)
    sums = None
    for t in range(tiles_here):
        one = slice(t, t + 1)
        terms = whole(
            grid, scale, user_block[one], item_block[one], stratum[one], context_ids[one],
            observed[t], core_tensor, user_factor, item_factor, context_factor,
        )
        sums = terms if sums is None else tuple(a + b for a, b in zip(sums, terms))
    core_grad, item_grad, context_grad, user_grad = hand_over(sums)
    return (core_grad, user_grad, item_grad, context_grad)


def solution(mesh):
    grid = Grid(mesh.shape["user"], mesh.shape["item"])
    both = ("user", "item")
    return jax.shard_map(
        functools.partial(local, grid),
        mesh=mesh,
        in_specs=(
            P(both, None, None, None),
            P(both),
            P(both),
            P(both),
            P(both, None),
            P(both, None),
            P("user", None),
            P("item", None),
            P(both, None),
        ),
        out_specs=(P(both, None), P(both, None), P(both, None), P(both, None)),
        check_vma=False,
    )
```
